256 devices in a mesh: grp: 2 (over y_lo), gy: 8 (over x, core), gz: 16 (over y_hi, z).
Axes of the slice: x: 4, y: 4 (y_hi: 2, y_lo: 2; y = y_hi * 2 + y_lo), z: 8, core: 2. Of those that a mesh axis runs over, the one named last changes fastest.
Arguments:
- offsets: float32 [2, 16, 128, 3, 128], P('grp', 'gy', 'gz'), may hold values from 0 to 1
- nbr_list: int32 [2, 16, 128, 9], P('grp', 'gy', 'gz'), may hold values from 0 to 8, as said below
- nbr_count: int32 [2, 16, 128], P('grp', 'gy', 'gz'), may hold values from 1 to 9, as said below
- source: float32 [2, 16, 128, 128], P('grp', 'gy', 'gz'), may hold values from -180 to 180
- start_p: float32 [2, 16, 128, 128], P('grp', 'gy', 'gz'), may hold values from -6 to 6
- guard_coef: float32 [2, 8, 16, 16, 128], P('grp', 'gy', 'gz'), may hold values from 10 to 100
- send_block: int32 [2, 8, 16, 8], P('grp', 'gy', 'gz'), may hold values from 0 to 15
- send_tile: int32 [2, 8, 16, 8], P('grp', 'gy', 'gz'), may hold values from 0 to 127
- send_guard: int32 [2, 8, 16, 8], P('grp', 'gy', 'gz'), may hold values from 0 to 15
- send_count: int32 [2, 8, 16], P('grp', 'gy', 'gz'), may hold values from 1 to 8, as said below
- interp: float32 [2, 8, 16, 8, 128, 128], P('grp', 'gy', 'gz'), may hold values from -0.5 to 0.5
Outputs:
- pressure: float32 [2, 16, 128, 128], P('grp', 'gy', 'gz')
The draws below stay inside these ranges and needn't reach their ends.
Inputs may be any that keep to these rules, and one draw needn't show every extreme that they name: `nbr_list`: the entries of one block's list are distinct slot codes. `nbr_count`: every draw has a block with all 9 slots live in each tile. `send_count`: every draw has, in some tile of each group, all 8 outgoing interpolations live.
All inputs are finite; a program needn't handle non-finite values.
Results may differ from the reference program's by a relative error of at most 0.0001.
Values sent between devices are 32-bit elements; how exact they have to be, the bound alone decides.
A program may use at most 64 MiB of HBM per device.

```python
import math
import jax
import jax.numpy as jnp
from jax import lax

PB = 128
SLOTS = 9
BY = 2
BZ = 8
GIN = 16
GOUT = 8
ITERS = 3
NYG = 16
NZG = 128
TILES = 128
N_GY = 8
N_GZ = 16


def draw_nbr_list(key, part):
    scores = jax.random.randint(key, (2, NYG, NZG, SLOTS), 0, 1 << 20) * 16 + jnp.arange(SLOTS, dtype=jnp.int32)
    return jnp.argsort(scores, axis=-1).astype(jnp.int32)


def draw_nbr_count(key, part):
    base = jax.random.randint(jax.random.fold_in(key, 1), (2, NYG, NZG), 1, SLOTS + 1)
    ny_tiles = NYG // BY
    nz_tiles = NZG // BZ
    chosen = jax.random.randint(jax.random.fold_in(key, 2), (2, ny_tiles, nz_tiles), 0, BY * BZ)
    chosen_grid = jnp.repeat(jnp.repeat(chosen, BY, axis=1), BZ, axis=2)
    rows_in = (jnp.arange(NYG, dtype=jnp.int32) % BY)[:, None]
    cols_in = (jnp.arange(NZG, dtype=jnp.int32) % BZ)[None, :]
    block_id = (rows_in * BZ + cols_in)[None, :, :]
    return jnp.where(block_id == chosen_grid, SLOTS, base).astype(jnp.int32)


def draw_send_count(key, part):
    ny_tiles = NYG // BY
    nz_tiles = NZG // BZ
    base = jax.random.randint(jax.random.fold_in(key, 3), (2, ny_tiles * nz_tiles), 1, GOUT + 1)
    chosen = jax.random.randint(jax.random.fold_in(key, 4), (2, 1), 0, ny_tiles * nz_tiles)
    position = jnp.arange(ny_tiles * nz_tiles, dtype=jnp.int32)[None, :]
    full = jnp.where(position == chosen, GOUT, base)
    return full.reshape(2, ny_tiles, nz_tiles).astype(jnp.int32)


def place_ends(values, key, low, high):
    shape = values.shape
    spot = [jax.random.randint(jax.random.fold_in(key, axis), (), 0, shape[axis]) for axis in range(len(shape))]
    values = values.at[tuple(spot)].set(low)
    longest = shape.index(max(shape))
    spot[longest] = (spot[longest] + 1) % shape[longest]
    return values.at[tuple(spot)].set(high)


def shard_levels(stream_key, shape, pieces, low, top_value):
    def one(dim, shards_of):
        draws = jax.random.uniform(jax.random.fold_in(jax.random.fold_in(stream_key, 6), dim), (shards_of,), jnp.float32, low / len(pieces), top_value / len(pieces))
        return jnp.repeat(jnp.exp(draws), shape[dim] // shards_of).reshape((-1,) + (1,) * (len(shape) - dim - 1))

    loudness = one(*pieces[0])
    for cut in pieces[1:]:
        loudness = loudness * one(*cut)
    return loudness


def gaussian(rng, extent, scale, reach, split=(), kind=jnp.bfloat16):
    loudness = shard_levels(rng, extent, split, -0.22, 0.18) if split else 1.0
    drawn = jax.random.normal(rng, extent, jnp.float32) * scale * loudness
    return jnp.minimum(jnp.maximum(drawn, -reach), reach).astype(kind)


def setup_inputs(seed: int = 0) -> dict:
    keys = jax.random.split(jax.random.key(seed), 12)
    offsets = jnp.clip(1.0 * jax.random.uniform(keys[0], (2, NYG, NZG, 3, PB), jnp.float32) ** shard_levels(keys[0], (2, NYG, NZG, 3, PB), ((0, 2), (1, 8), (2, 16)), -0.2, 0.2), 0.0, 1.0)
    nbr_list = draw_nbr_list(jax.random.fold_in(keys[11], 71), 0)
    nbr_count = draw_nbr_count(jax.random.fold_in(keys[11], 71), 0)
    source = gaussian(keys[3], (2, NYG, NZG, PB), 30.0, 180.0, ((0, 2), (1, 8), (2, 16)), jnp.float32)
    start_p = gaussian(keys[4], (2, NYG, NZG, PB), 1.0, 6.0, ((0, 2), (1, 8), (2, 16)), jnp.float32)
    guard_coef = jnp.clip(jnp.exp(math.log(100.0) - 2.3025851 * jax.random.uniform(keys[5], (2, N_GY, N_GZ, GIN, PB), jnp.float32) ** shard_levels(keys[5], (2, N_GY, N_GZ, GIN, PB), ((0, 2), (1, 8), (2, 16)), -0.2, 0.2)), 10.0, 100.0)
    send_block = place_ends(jax.random.randint(keys[6], (2, N_GY, N_GZ, GOUT), 0, BY * BZ), jax.random.fold_in(keys[6], 1), 0, (BY * BZ) - 1).astype(jnp.int32)
    send_tile = place_ends(jax.random.randint(keys[7], (2, N_GY, N_GZ, GOUT), 0, TILES), jax.random.fold_in(keys[7], 1), 0, TILES - 1).astype(jnp.int32)
    send_guard = place_ends(jax.random.randint(keys[8], (2, N_GY, N_GZ, GOUT), 0, GIN), jax.random.fold_in(keys[8], 1), 0, GIN - 1).astype(jnp.int32)
    send_count = draw_send_count(jax.random.fold_in(keys[11], 71), 0)
    interp = gaussian(keys[10], (2, N_GY, N_GZ, GOUT, PB, PB), PB ** -0.5, 0.5, ((0, 2), (1, 8), (2, 16)), jnp.float32)
    return dict(offsets=offsets, nbr_list=nbr_list, nbr_count=nbr_count, source=source, start_p=start_p, guard_coef=guard_coef, send_block=send_block, send_tile=send_tile, send_guard=send_guard, send_count=send_count, interp=interp)


KERNEL_WIDTH = 0.5


def pair_sums(own_rows, near_rows, near_press, step_y, step_z):
    shift_vec = jnp.array([0.0, step_y, step_z], jnp.float32)

    def one_row(items):
        own, near, press = items
        diff = own[..., :, :, None] - (near[..., :, None, :] + shift_vec[:, None, None])
        weight = jnp.exp(-jnp.sum(diff * diff, axis=-3) / KERNEL_WIDTH)
        return jnp.sum(weight * press[..., None, :], axis=-1), jnp.sum(weight, axis=-1)

    moved = (jnp.moveaxis(own_rows, 1, 0), jnp.moveaxis(near_rows, 1, 0), jnp.moveaxis(near_press, 1, 0))
    weighted, totals = lax.map(one_row, moved)
    return jnp.moveaxis(weighted, 0, 1), jnp.moveaxis(totals, 0, 1)


def reference(offsets, nbr_list, nbr_count, source, start_p, guard_coef, send_block, send_tile, send_guard, send_count, interp):
    ny_tiles = NYG // BY
    nz_tiles = NZG // BZ
    tiles_all = ny_tiles * nz_tiles
    blocks = BY * BZ
    live = jnp.arange(SLOTS, dtype=jnp.int32)[None, None, None, :] < nbr_count[..., None]
    pressure = start_p
    coef_full = jnp.concatenate([guard_coef, jnp.zeros((2, ny_tiles, nz_tiles, blocks - GIN, PB), jnp.float32)], axis=3)
    coef_grid = coef_full.reshape(2, ny_tiles, nz_tiles, BY, BZ, PB).transpose(0, 1, 3, 2, 4, 5).reshape(2, NYG, NZG, PB)
    slot_live = jnp.arange(GOUT, dtype=jnp.int32)[None, None, None, :] < send_count[..., None]
    dest_code = (send_tile * GIN + send_guard).reshape(2, tiles_all * GOUT)
    onehot = (dest_code[:, :, None] == jnp.arange(tiles_all * GIN, dtype=jnp.int32)[None, None, :]).astype(jnp.float32)
    for sweep_no in range(ITERS):
        numer = jnp.zeros((2, NYG, NZG, PB), jnp.float32)
        denom = jnp.zeros((2, NYG, NZG, PB), jnp.float32)
        for step_y in (-1, 0, 1):
            for step_z in (-1, 0, 1):
                slot_code = 3 * (step_y + 1) + (step_z + 1)
                near_off = jnp.roll(offsets, (-step_y, -step_z), axis=(1, 2))
                near_p = jnp.roll(pressure, (-step_y, -step_z), axis=(1, 2))
                weighted, totals = pair_sums(offsets, near_off, near_p, float(step_y), float(step_z))
                active = jnp.sum(((nbr_list == slot_code) & live).astype(jnp.float32), axis=-1)[..., None]
                numer = numer + active * weighted
                denom = denom + active * totals
        tile_blocks = pressure.reshape(2, ny_tiles, BY, nz_tiles, BZ, PB).transpose(0, 1, 3, 2, 4, 5).reshape(2, ny_tiles, nz_tiles, blocks, PB)
        chosen = jnp.take_along_axis(tile_blocks, send_block[..., None], axis=3)
        values = jnp.einsum('gyzsij,gyzsj->gyzsi', interp, chosen, precision=lax.Precision.HIGHEST)
        values = values * slot_live[..., None].astype(jnp.float32)
        flat_values = values.reshape(2, tiles_all * GOUT, PB)
        table = jnp.einsum('gsd,gsi->gdi', onehot, flat_values, precision=lax.Precision.HIGHEST)
        guard_p = table[::-1].reshape(2, ny_tiles, nz_tiles, GIN, PB)
        guard_full = jnp.concatenate([guard_p, jnp.zeros((2, ny_tiles, nz_tiles, blocks - GIN, PB), jnp.float32)], axis=3)
        guard_grid = guard_full.reshape(2, ny_tiles, nz_tiles, BY, BZ, PB).transpose(0, 1, 3, 2, 4, 5).reshape(2, NYG, NZG, PB)
        pressure = (numer + coef_grid * guard_grid - source) / (denom + coef_grid + 1.0)
    return pressure
```

```python
import functools
import math

import jax
import jax.numpy as jnp
from jax import lax
from jax.experimental import pallas as pl
from jax.experimental.pallas import tpu as pltpu
from jax.sharding import PartitionSpec as P

PB = 128
SLOTS = 9
ITERS = 3
KERNEL_WIDTH = 0.5
MESH = pl.DeviceIdType.MESH
KAPPA = math.sqrt(1.0 / (KERNEL_WIDTH * math.log(2.0)))
OFF = -1.0e4


def kernel(
    n_gy,
    n_gz,
    off_ref,
    list_ref,
    cnt_ref,
    src_ref,
    p_ref,
    gc_ref,
    sb_ref,
    st_ref,
    sg_ref,
    sc_ref,
    interp_ref,
    out_ref,
    ext0,
    own8,
    pext,
    pden,
    wts,
    mask,
    first,
    later,
    got_first,
    got,
    buckets,
    got_buckets,
    onehot,
    num,
    den,
    h_send,
    h_recv,
    g_send,
    g_recv,
    r_send,
    r_recv,
):
    g = lax.axis_index("grp")
    y = lax.axis_index("gy")
    z = lax.axis_index("gz")
    rows_y, cols_z = off_ref.shape[1], off_ref.shape[2]
    guards = gc_ref.shape[3]
    slots_out = sb_ref.shape[3]

    def at(gg, dy, dz):
        return (gg, lax.rem(y + dy + n_gy, n_gy), lax.rem(z + dz + n_gz, n_gz))

    partners = {(1, 0, o) for o in range(n_gz)}
    partners |= {(0, o, 0) for o in range(1, n_gy)}
    partners |= {
        (0, a % n_gy, b % n_gz) for a in (-1, 0, 1) for b in (-1, 0, 1) if (a, b) != (0, 0)
    }
    partners = sorted(partners)

    barrier = pltpu.get_barrier_semaphore()
    for flip, dy, dz in partners:
        pl.semaphore_signal(
            barrier,
            inc=1,
            device_id=at(1 - g if flip else g, dy, dz),
            device_id_type=MESH,
        )

    sides = []
    for dy in (-1, 0, 1):
        for dz in (-1, 0, 1):
            if (dy, dz) == (0, 0):
                continue
            ys = {-1: (1, 1), 0: (1, rows_y), 1: (rows_y, 1)}[dy]
            zs = {-1: (1, 1), 0: (1, cols_z), 1: (cols_z, 1)}[dz]
            yd = {-1: rows_y + 1, 0: 1, 1: 0}[dy]
            zd = {-1: cols_z + 1, 0: 1, 1: 0}[dz]
            sides.append((dy, dz, ys, zs, yd, zd))

    def send_halo(buf, sweep):
        for dy, dz, ys, zs, yd, zd in sides:
            pltpu.make_async_remote_copy(
                src_ref=buf.at[pl.ds(ys[0], ys[1]), pl.ds(zs[0], zs[1])],
                dst_ref=buf.at[pl.ds(yd, ys[1]), pl.ds(zd, zs[1])],
                send_sem=h_send.at[sweep],
                recv_sem=h_recv.at[sweep],
                device_id=at(g, dy, dz),
                device_id_type=MESH,
            ).start()

    rim = 2 * cols_z + 2 * rows_y + 4

    def rim_wait(buf, sem):
        part = buf.at[pl.ds(0, rim // cols_z), pl.ds(0, cols_z)]
        pltpu.make_async_copy(part, part, sem).wait()

    def send_values(src, dst, sweep):
        order = sorted(range(n_gz), key=lambda o: -min(o, n_gz - o))
        for o in order:
            pltpu.make_async_remote_copy(
                src_ref=src,
                dst_ref=dst.at[o],
                send_sem=g_send.at[sweep],
                recv_sem=g_recv.at[sweep],
                device_id=at(1 - g, 0, o),
                device_id_type=MESH,
            ).start()

    def send_buckets(sweep):
        order = sorted(range(1, n_gy), key=lambda o: -min(o, n_gy - o))
        for o in order:
            to = lax.rem(y + o, n_gy)
            pltpu.make_async_remote_copy(
                src_ref=buckets.at[sweep, to],
                dst_ref=got_buckets.at[sweep, o - 1],
                send_sem=r_send.at[sweep],
                recv_sem=r_recv.at[sweep],
                device_id=at(g, o, 0),
                device_id_type=MESH,
            ).start()

    def whole_wait(ref, sem):
        pltpu.make_async_copy(ref, ref, sem).wait()

    row_id = lax.broadcasted_iota(jnp.int32, (PB, PB), 0)
    lane_id = lax.broadcasted_iota(jnp.int32, (PB, PB), 1)
    eye = row_id == lane_id

    def row_sums(acc):
        total = jnp.sum(acc, axis=1, keepdims=True)
        return jnp.sum(jnp.where(eye, total, 0.0), axis=0, keepdims=True)

    def interpolate(dst):
        for s in range(slots_out):
            press = pden[pl.ds(sb_ref[0, 0, 0, s], 1), :]
            dst[pl.ds(s, 1), :] = row_sums(interp_ref[0, 0, 0, s] * press)

    for a in range(rows_y):
        for b in range(cols_z):
            scaled = (off_ref[0, a, b] - 0.5) * (2.0 * KAPPA)
            ext0[1 + a, 1 + b, pl.ds(0, 3), :] = scaled
            ext0[1 + a, 1 + b, pl.ds(3, 1), :] = p_ref[0, a, pl.ds(b, 1), :]
            own8[a, b, pl.ds(0, 3), :] = scaled * 0.5
        pden[pl.ds(a * cols_z, cols_z), :] = p_ref[0, a]

    interpolate(first)
    codes = jnp.full((slots_out, PB), -1, jnp.int32)
    slot_row = lax.broadcasted_iota(jnp.int32, (slots_out, PB), 0)
    for s in range(slots_out):
        codes = jnp.where(slot_row == s, st_ref[0, 0, 0, s] * guards + sg_ref[0, 0, 0, s], codes)
    codes = jnp.where(slot_row < sc_ref[0, 0, 0], codes, -1)
    first[pl.ds(slots_out, slots_out), :] = codes.astype(jnp.float32)

    pl.semaphore_wait(barrier, len(partners))
    send_values(first, got_first, 0)
    send_halo(ext0, 0)

    for a in range(rows_y):
        lanes = lax.broadcasted_iota(jnp.int32, (cols_z, cols_z), 1)
        subs = lax.broadcasted_iota(jnp.int32, (cols_z, cols_z), 0)
        counts = jnp.sum(
            jnp.where(lanes == subs, cnt_ref[0, pl.ds(a, 1), :], 0).astype(jnp.float32),
            axis=1,
            keepdims=True,
        )
        places = lax.broadcasted_iota(jnp.int32, (cols_z, SLOTS), 1).astype(jnp.float32)
        for c in range(SLOTS):
            hit = (list_ref[0, a] == c) & (places < counts)
            active = jnp.sum(jnp.where(hit, 1.0, 0.0), axis=1, keepdims=True)
            mask[c, a] = jnp.broadcast_to((1.0 - active) * OFF, (cols_z, PB))

    def own_columns(a, b):
        cols = jnp.transpose(own8[a, b])
        cx = jnp.broadcast_to(cols[:, 0:1], (PB, PB))
        cy = jnp.broadcast_to(cols[:, 1:2], (PB, PB))
        cz = jnp.broadcast_to(cols[:, 2:3], (PB, PB))
        return cx, cy, cz, -(cx * cx + cy * cy + cz * cz)

    def make_weights(a, b, pairs):
        cx, cy, cz, cn = own_columns(a, b)
        for dy, dz in pairs:
            c = 3 * (dy + 1) + (dz + 1)
            near = ext0[1 + a + dy, 1 + b + dz]
            rx = near[0:1]
            ry = near[1:2] + 2.0 * KAPPA * dy
            rz = near[2:3] + 2.0 * KAPPA * dz
            rn = mask[c, a, pl.ds(b, 1), :] - 0.25 * (rx * rx + ry * ry + rz * rz)
            wts[a, b, c] = jnp.exp2((cn + rn) + (cx * rx + cy * ry) + cz * rz)

    all_dz = (-1, 0, 1)

    def inner(b, carry):
        for a in range(rows_y):
            dys = [dy for dy in (-1, 0, 1) if 0 <= a + dy < rows_y]
            make_weights(a, b, [(dy, dz) for dy in dys for dz in all_dz])
        return carry

    def outer(b, carry):
        for a in range(rows_y):
            dys = [dy for dy in (-1, 0, 1) if not 0 <= a + dy < rows_y]
            make_weights(a, b, [(dy, dz) for dy in dys for dz in all_dz])
        return carry

    def ends(t, carry):
        for a in range(rows_y):
            make_weights(
                a, t * (cols_z - 1), [(dy, dz) for dy in (-1, 0, 1) for dz in all_dz]
            )
        return carry

    def deliver(values, sweep):
        hi = values.astype(jnp.bfloat16)
        rest = values - hi.astype(jnp.float32)
        mid = rest.astype(jnp.bfloat16)
        low = (rest - mid.astype(jnp.float32)).astype(jnp.bfloat16)
        sel = onehot[...]
        total = jnp.dot(sel, hi, preferred_element_type=jnp.float32)
        total += jnp.dot(sel, mid, preferred_element_type=jnp.float32)
        total += jnp.dot(sel, low, preferred_element_type=jnp.float32)
        buckets[sweep] = total.reshape(n_gy, guards, PB)
        send_buckets(sweep)

    def sums(near_row, with_den):
        def body(b, carry):
            rows = [[near_row(e, b + k) for k in range(3)] for e in range(rows_y + 2)]
            for a in range(rows_y):
                acc = None
                tot = None
                for c in range(SLOTS):
                    w = wts[a, b, c]
                    part = w * rows[a + c // 3][c % 3]
                    acc = part if acc is None else acc + part
                    if with_den:
                        tot = w if tot is None else tot + w
                num[a, pl.ds(b, 1), :] = row_sums(acc)
                if with_den:
                    den[a, pl.ds(b, 1), :] = row_sums(tot)
            return carry

        lax.fori_loop(0, cols_z, body, 0)

    lax.fori_loop(1, cols_z - 1, inner, 0)

    whole_wait(got_first, g_recv.at[0])
    entries = n_gz * slots_out
    dest = n_gy * guards
    code_rows = got_first[:, pl.ds(slots_out, slots_out), :].reshape(entries, PB)[:, :dest]
    lane = lax.broadcasted_iota(jnp.int32, (entries, dest), 1)
    wanted = (lane // guards * n_gz + z) * guards + lax.rem(lane, guards)
    hits = jnp.where(code_rows == wanted.astype(jnp.float32), 1.0, 0.0)
    onehot[...] = jnp.transpose(hits).astype(jnp.bfloat16)
    deliver(got_first[:, pl.ds(0, slots_out), :].reshape(entries, PB), 0)

    rim_wait(ext0, h_recv.at[0])
    lax.fori_loop(1, cols_z - 1, outer, 0)
    lax.fori_loop(0, 2, ends, 0)

    sums(lambda e, k: ext0[e, k, pl.ds(3, 1), :], True)
    coef = gc_ref[0, 0, 0].reshape(rows_y, cols_z, PB)
    scale = 1.0 / (den[...] + coef + 1.0)

    for sweep in range(ITERS):
        base = num[...] - src_ref[0]
        whole_wait(got_buckets.at[sweep], r_recv.at[sweep])
        mine = buckets[sweep, y]
        for o in range(n_gy - 1):
            mine = mine + got_buckets[sweep, o]
        new = (base + coef * mine.reshape(rows_y, cols_z, PB)) * scale
        if sweep == ITERS - 1:
            out_ref[0] = new
            break
        pden[...] = new.reshape(rows_y * cols_z, PB)
        interpolate(later.at[sweep])
        send_values(later.at[sweep], got.at[sweep], sweep + 1)
        press = pext.at[sweep]
        for a in range(rows_y):
            for b in range(cols_z):
                press[1 + a, 1 + b] = new[a, b : b + 1]
        send_halo(press, sweep + 1)
        rim_wait(press, h_recv.at[sweep + 1])
        whole_wait(got.at[sweep], g_recv.at[sweep + 1])
        deliver(got[sweep].reshape(entries, PB), sweep + 1)
        sums(lambda e, k: press[e, k], False)

    rim_wait(ext0, h_send.at[0])
    whole_wait(got_first, g_send.at[0])
    for sweep in range(ITERS):
        whole_wait(got_buckets.at[sweep], r_send.at[sweep])
        if sweep:
            rim_wait(pext.at[sweep - 1], h_send.at[sweep])
            whole_wait(got.at[sweep - 1], g_send.at[sweep])


def local(n_gy, n_gz, *args):
    offsets, guard_coef, send_block = args[0], args[5], args[6]
    rows_y, cols_z = offsets.shape[1:3]
    guards = guard_coef.shape[3]
    slots_out = send_block.shape[3]
    f32 = jnp.float32
    vmem = pl.BlockSpec(memory_space=pltpu.VMEM)
    smem = pl.BlockSpec(memory_space=pltpu.SMEM)
    dma = pltpu.SemaphoreType.DMA((ITERS,))
    return pl.pallas_call(
        functools.partial(kernel, n_gy, n_gz),
        out_shape=jax.ShapeDtypeStruct((1, rows_y, cols_z, PB), f32),
        in_specs=[vmem] * 6 + [smem] * 4 + [vmem],
        out_specs=vmem,
        scratch_shapes=[
            pltpu.VMEM((rows_y + 2, cols_z + 2, 4, PB), f32),
            pltpu.VMEM((rows_y, cols_z, 8, PB), f32),
            pltpu.VMEM((ITERS - 1, rows_y + 2, cols_z + 2, 1, PB), f32),
            pltpu.VMEM((rows_y * cols_z, PB), f32),
            pltpu.VMEM((rows_y, cols_z, SLOTS, PB, PB), f32),
            pltpu.VMEM((SLOTS, rows_y, cols_z, PB), f32),
            pltpu.VMEM((2 * slots_out, PB), f32),
            pltpu.VMEM((ITERS - 1, slots_out, PB), f32),
            pltpu.VMEM((n_gz, 2 * slots_out, PB), f32),
            pltpu.VMEM((ITERS - 1, n_gz, slots_out, PB), f32),
            pltpu.VMEM((ITERS, n_gy, guards, PB), f32),
            pltpu.VMEM((ITERS, n_gy - 1, guards, PB), f32),
            pltpu.VMEM((n_gy * guards, n_gz * slots_out), jnp.bfloat16),
            pltpu.VMEM((rows_y, cols_z, PB), f32),
            pltpu.VMEM((rows_y, cols_z, PB), f32),
            dma,
            dma,
            dma,
            dma,
            dma,
            dma,
        ],
        compiler_params=pltpu.CompilerParams(
            collective_id=0, has_side_effects=True, vmem_limit_bytes=32 * 1024 * 1024
        ),
    )(*args)


def solution(mesh):
    placed = (
        P("grp", "gy", "gz", None, None),
        P("grp", "gy", "gz", None),
        P("grp", "gy", "gz"),
        P("grp", "gy", "gz", None),
        P("grp", "gy", "gz", None),
        P("grp", "gy", "gz", None, None),
        P("grp", "gy", "gz", None),
        P("grp", "gy", "gz", None),
        P("grp", "gy", "gz", None),
        P("grp", "gy", "gz"),
        P("grp", "gy", "gz", None, None, None),
    )
    return jax.shard_map(
        functools.partial(local, mesh.shape["gy"], mesh.shape["gz"]),
        mesh=mesh,
        in_specs=placed,
        out_specs=P("grp", "gy", "gz", None),
        check_vma=False,
    )
```

```python
import functools
import math

import jax
import jax.numpy as jnp
from jax import lax
from jax.experimental import pallas as pl
from jax.experimental.pallas import tpu as pltpu
from jax.sharding import PartitionSpec as P

PB = 128
SLOTS = 9
ITERS = 3
KERNEL_WIDTH = 0.5
MESH = pl.DeviceIdType.MESH
KAPPA = math.sqrt(1.0 / (KERNEL_WIDTH * math.log(2.0)))
OFF = -1.0e4


def kernel(
    n_gy,
    n_gz,
    *refs,
):
    sources, out_ref, held, rest = refs[:11], refs[11], refs[12:23], refs[23:]
    off_ref, list_ref, cnt_ref, src_ref, p_ref, gc_ref = held[:6]
    sb_ref, st_ref, sg_ref, sc_ref, interp_ref = held[6:]
    (
    ext0,
    own8,
    pext,
    pden,
    wts,
    mask,
    first,
    later,
    got_first,
    got,
    buckets,
    got_buckets,
    onehot,
    num,
    den,
    h_send,
    h_recv,
    g_send,
    g_recv,
    r_send,
    r_recv,
    in_sem,
    ) = rest
    g = lax.axis_index("grp")
    y = lax.axis_index("gy")
    z = lax.axis_index("gz")
    rows_y, cols_z = off_ref.shape[1], off_ref.shape[3]
    n_near = n_gz // 2
    half, near = z // n_near, lax.rem(z, n_near)
    guards = gc_ref.shape[3]
    slots_out = sb_ref.shape[3]

    def at(gg, dy, dz):
        return (gg, lax.rem(y + dy + n_gy, n_gy), lax.rem(z + dz + n_gz, n_gz))

    stage1 = sorted(
        ((o, f) for o in range(n_gy) for f in range(2)),
        key=lambda of: -(min(of[0] // 2, (n_gy - of[0] + 1) // 2) + 0.1 * (of[0] % 2)),
    )
    stage2 = sorted(range(1, n_near), key=lambda o: -min(o, n_near - o))

    def at1(o, f):
        return (1 - g, y ^ o, (half ^ f) * n_near + near)

    def at2(o):
        return (g, y, half * n_near + (near ^ o))

    neighbours = [
        (a, b) for a in (-1, 0, 1) for b in (-1, 0, 1) if (a, b) != (0, 0)
    ]

    copies = [
        pltpu.make_async_copy(src, dst, in_sem.at[i])
        for i, (src, dst) in enumerate(zip(sources, held))
    ]
    copies[10].start()
    barrier = pltpu.get_barrier_semaphore()
    people = [at1(*of) for of in stage1] + [at2(o) for o in stage2]
    people += [at(g, *ab) for ab in neighbours]
    for who in people:
        pl.semaphore_signal(barrier, inc=1, device_id=who, device_id_type=MESH)
    for i in (4, 6, 0, 7, 8, 9, 1, 2, 3, 5):
        copies[i].start()

    sides = []
    for dy in (-1, 0, 1):
        for dz in (-1, 0, 1):
            if (dy, dz) == (0, 0):
                continue
            ys = {-1: (1, 1), 0: (1, rows_y), 1: (rows_y, 1)}[dy]
            zs = {-1: (1, 1), 0: (1, cols_z), 1: (cols_z, 1)}[dz]
            yd = {-1: rows_y + 1, 0: 1, 1: 0}[dy]
            zd = {-1: cols_z + 1, 0: 1, 1: 0}[dz]
            sides.append((dy, dz, ys, zs, yd, zd))

    def send_halo(buf, sweep):
        for dy, dz, ys, zs, yd, zd in sides:
            pltpu.make_async_remote_copy(
                src_ref=buf.at[pl.ds(ys[0], ys[1]), pl.ds(zs[0], zs[1])],
                dst_ref=buf.at[pl.ds(yd, ys[1]), pl.ds(zd, zs[1])],
                send_sem=h_send.at[sweep],
                recv_sem=h_recv.at[sweep],
                device_id=at(g, dy, dz),
                device_id_type=MESH,
            ).start()

    rim = 2 * cols_z + 2 * rows_y + 4

    def rim_wait(buf, sem):
        part = buf.at[pl.ds(0, rim // cols_z), pl.ds(0, cols_z)]
        pltpu.make_async_copy(part, part, sem).wait()

    def send_values(src, dst, sweep):
        for o, f in stage1:
            pltpu.make_async_remote_copy(
                src_ref=src,
                dst_ref=dst.at[2 * o + f],
                send_sem=g_send.at[sweep],
                recv_sem=g_recv.at[sweep],
                device_id=at1(o, f),
                device_id_type=MESH,
            ).start()

    def send_buckets(sweep):
        for o in stage2:
            pltpu.make_async_remote_copy(
                src_ref=buckets.at[sweep, near ^ o],
                dst_ref=got_buckets.at[sweep, o - 1],
                send_sem=r_send.at[sweep],
                recv_sem=r_recv.at[sweep],
                device_id=at2(o),
                device_id_type=MESH,
            ).start()

    def whole_wait(ref, sem):
        pltpu.make_async_copy(ref, ref, sem).wait()

    row_id = lax.broadcasted_iota(jnp.int32, (PB, PB), 0)
    lane_id = lax.broadcasted_iota(jnp.int32, (PB, PB), 1)
    eye = row_id == lane_id

    def row_sums(acc):
        total = jnp.sum(acc, axis=1, keepdims=True)
        return jnp.sum(jnp.where(eye, total, 0.0), axis=0, keepdims=True)

    def interpolate(dst):
        for s in range(slots_out):
            press = pden[pl.ds(sb_ref[0, 0, 0, s], 1), :]
            dst[pl.ds(s, 1), :] = row_sums(interp_ref[0, 0, 0, s] * press)

    for i in (4, 6):
        copies[i].wait()
    for a in range(rows_y):
        pden[pl.ds(a * cols_z, cols_z), :] = p_ref[0, a]
    copies[10].wait()
    interpolate(first)
    for i in (7, 8, 9):
        copies[i].wait()
    codes = jnp.full((slots_out, PB), -1, jnp.int32)
    slot_row = lax.broadcasted_iota(jnp.int32, (slots_out, PB), 0)
    for s in range(slots_out):
        codes = jnp.where(slot_row == s, st_ref[0, 0, 0, s] * guards + sg_ref[0, 0, 0, s], codes)
    codes = jnp.where(slot_row < sc_ref[0, 0, 0], codes, -1)
    first[pl.ds(slots_out, slots_out), :] = codes.astype(jnp.float32)

    copies[0].wait()
    for a in range(rows_y):
        for k in range(3):
            scaled = (off_ref[0, a, k] - 0.5) * (2.0 * KAPPA)
            for b in range(cols_z):
                ext0[1 + a, 1 + b, pl.ds(k, 1), :] = scaled[b : b + 1]
                own8[a, b, pl.ds(k, 1), :] = 0.5 * scaled[b : b + 1]
        for b in range(cols_z):
            ext0[1 + a, 1 + b, pl.ds(3, 1), :] = p_ref[0, a, pl.ds(b, 1), :]

    pl.semaphore_wait(barrier, len(people))
    send_values(first, got_first, 0)
    send_halo(ext0, 0)
    for i in (1, 2, 3, 5):
        copies[i].wait()

    for a in range(rows_y):
        lanes = lax.broadcasted_iota(jnp.int32, (cols_z, cols_z), 1)
        subs = lax.broadcasted_iota(jnp.int32, (cols_z, cols_z), 0)
        counts = jnp.sum(
            jnp.where(lanes == subs, cnt_ref[0, pl.ds(a, 1), :], 0).astype(jnp.float32),
            axis=1,
            keepdims=True,
        )
        places = lax.broadcasted_iota(jnp.int32, (cols_z, SLOTS), 1).astype(jnp.float32)
        for c in range(SLOTS):
            hit = (list_ref[0, a] == c) & (places < counts)
            active = jnp.sum(jnp.where(hit, 1.0, 0.0), axis=1, keepdims=True)
            mask[c, a] = jnp.broadcast_to((1.0 - active) * OFF, (cols_z, PB))

    def own_columns(a, b):
        cols = jnp.transpose(own8[a, b])
        cx = jnp.broadcast_to(cols[:, 0:1], (PB, PB))
        cy = jnp.broadcast_to(cols[:, 1:2], (PB, PB))
        cz = jnp.broadcast_to(cols[:, 2:3], (PB, PB))
        return cx, cy, cz, -(cx * cx + cy * cy + cz * cz)

    def make_weights(a, b, pairs):
        cx, cy, cz, cn = own_columns(a, b)
        for dy, dz in pairs:
            c = 3 * (dy + 1) + (dz + 1)
            near = ext0[1 + a + dy, 1 + b + dz]
            rx = near[0:1]
            ry = near[1:2] + 2.0 * KAPPA * dy
            rz = near[2:3] + 2.0 * KAPPA * dz
            rn = mask[c, a, pl.ds(b, 1), :] - 0.25 * (rx * rx + ry * ry + rz * rz)
            wts[a, b, c] = jnp.exp2((cn + rn) + (cx * rx + cy * ry) + cz * rz)

    all_dz = (-1, 0, 1)

    def inner(b, carry):
        for a in range(rows_y):
            dys = [dy for dy in (-1, 0, 1) if 0 <= a + dy < rows_y]
            make_weights(a, b, [(dy, dz) for dy in dys for dz in all_dz])
        return carry

    def outer(b, carry):
        for a in range(rows_y):
            dys = [dy for dy in (-1, 0, 1) if not 0 <= a + dy < rows_y]
            make_weights(a, b, [(dy, dz) for dy in dys for dz in all_dz])
        return carry

    def ends(t, carry):
        for a in range(rows_y):
            make_weights(
                a, t * (cols_z - 1), [(dy, dz) for dy in (-1, 0, 1) for dz in all_dz]
            )
        return carry

    def deliver(values, sweep):
        hi = values.astype(jnp.bfloat16)
        rest = values - hi.astype(jnp.float32)
        mid = rest.astype(jnp.bfloat16)
        low = (rest - mid.astype(jnp.float32)).astype(jnp.bfloat16)
        sel = onehot[...]
        total = jnp.dot(sel, hi, preferred_element_type=jnp.float32)
        total += jnp.dot(sel, mid, preferred_element_type=jnp.float32)
        total += jnp.dot(sel, low, preferred_element_type=jnp.float32)
        buckets[sweep] = total.reshape(n_near, guards, PB)
        send_buckets(sweep)

    def sums(near_row, with_den):
        def body(b, carry):
            rows = [[near_row(e, b + k) for k in range(3)] for e in range(rows_y + 2)]
            for a in range(rows_y):
                acc = None
                tot = None
                for c in range(SLOTS):
                    w = wts[a, b, c]
                    part = w * rows[a + c // 3][c % 3]
                    acc = part if acc is None else acc + part
                    if with_den:
                        tot = w if tot is None else tot + w
                num[a, pl.ds(b, 1), :] = row_sums(acc)
                if with_den:
                    den[a, pl.ds(b, 1), :] = row_sums(tot)
            return carry

        lax.fori_loop(0, cols_z, body, 0)

    lax.fori_loop(1, cols_z - 1, inner, 0)
    rim_wait(ext0, h_recv.at[0])
    middle = 1 + (cols_z - 2) // 2
    lax.fori_loop(1, middle, outer, 0)

    whole_wait(got_first, g_recv.at[0])
    entries = 2 * n_gy * slots_out
    dest = n_near * guards
    code_rows = got_first[:, pl.ds(slots_out, slots_out), :].reshape(entries, PB)[:, :dest]
    lane = lax.broadcasted_iota(jnp.int32, (entries, dest), 1)
    wanted = (y * n_gz + half * n_near) * guards + lane
    hits = jnp.where(code_rows == wanted.astype(jnp.float32), 1.0, 0.0)
    onehot[...] = jnp.transpose(hits).astype(jnp.bfloat16)
    deliver(got_first[:, pl.ds(0, slots_out), :].reshape(entries, PB), 0)

    lax.fori_loop(middle, cols_z - 1, outer, 0)
    lax.fori_loop(0, 2, ends, 0)

    sums(lambda e, k: ext0[e, k, pl.ds(3, 1), :], True)
    coef = gc_ref[0, 0, 0].reshape(rows_y, cols_z, PB)
    scale = 1.0 / (den[...] + coef + 1.0)

    for sweep in range(ITERS):
        base = num[...] - src_ref[0]
        whole_wait(got_buckets.at[sweep], r_recv.at[sweep])
        mine = buckets[sweep, near]
        for o in range(n_near - 1):
            mine = mine + got_buckets[sweep, o]
        new = (base + coef * mine.reshape(rows_y, cols_z, PB)) * scale
        if sweep == ITERS - 1:
            out_ref[0] = new
            break
        pden[...] = new.reshape(rows_y * cols_z, PB)
        interpolate(later.at[sweep])
        send_values(later.at[sweep], got.at[sweep], sweep + 1)
        press = pext.at[sweep]
        for a in range(rows_y):
            for b in range(cols_z):
                press[1 + a, 1 + b] = new[a, b : b + 1]
        send_halo(press, sweep + 1)
        rim_wait(press, h_recv.at[sweep + 1])
        whole_wait(got.at[sweep], g_recv.at[sweep + 1])
        deliver(got[sweep].reshape(entries, PB), sweep + 1)
        sums(lambda e, k: press[e, k], False)

    rim_wait(ext0, h_send.at[0])
    whole_wait(got_first, g_send.at[0])
    for sweep in range(ITERS):
        whole_wait(got_buckets.at[sweep], r_send.at[sweep])
        if sweep:
            rim_wait(pext.at[sweep - 1], h_send.at[sweep])
            whole_wait(got.at[sweep - 1], g_send.at[sweep])


def local(n_gy, n_gz, *args):
    args = (jnp.swapaxes(args[0], 2, 3),) + args[1:]
    guard_coef, send_block = args[5], args[6]
    rows_y, cols_z = args[3].shape[1:3]
    guards = guard_coef.shape[3]
    slots_out = send_block.shape[3]
    n_near = n_gz // 2
    f32 = jnp.float32
    dma = pltpu.SemaphoreType.DMA((ITERS,))
    spaces = [pltpu.VMEM] * 6 + [pltpu.SMEM] * 4 + [pltpu.VMEM]
    return pl.pallas_call(
        functools.partial(kernel, n_gy, n_gz),
        out_shape=jax.ShapeDtypeStruct((1, rows_y, cols_z, PB), f32),
        in_specs=[pl.BlockSpec(memory_space=pl.ANY)] * len(args),
        out_specs=pl.BlockSpec(memory_space=pltpu.VMEM),
        scratch_shapes=[space(a.shape, a.dtype) for space, a in zip(spaces, args)]
        + [
            pltpu.VMEM((rows_y + 2, cols_z + 2, 4, PB), f32),
            pltpu.VMEM((rows_y, cols_z, 8, PB), f32),
            pltpu.VMEM((ITERS - 1, rows_y + 2, cols_z + 2, 1, PB), f32),
            pltpu.VMEM((rows_y * cols_z, PB), f32),
            pltpu.VMEM((rows_y, cols_z, SLOTS, PB, PB), f32),
            pltpu.VMEM((SLOTS, rows_y, cols_z, PB), f32),
            pltpu.VMEM((2 * slots_out, PB), f32),
            pltpu.VMEM((ITERS - 1, slots_out, PB), f32),
            pltpu.VMEM((2 * n_gy, 2 * slots_out, PB), f32),
            pltpu.VMEM((ITERS - 1, 2 * n_gy, slots_out, PB), f32),
            pltpu.VMEM((ITERS, n_near, guards, PB), f32),
            pltpu.VMEM((ITERS, n_near - 1, guards, PB), f32),
            pltpu.VMEM((n_near * guards, 2 * n_gy * slots_out), jnp.bfloat16),
            pltpu.VMEM((rows_y, cols_z, PB), f32),
            pltpu.VMEM((rows_y, cols_z, PB), f32),
            dma,
            dma,
            dma,
            dma,
            dma,
            dma,
            pltpu.SemaphoreType.DMA((len(args),)),
        ],
        compiler_params=pltpu.CompilerParams(
            collective_id=0, has_side_effects=True, vmem_limit_bytes=60 * 1024 * 1024
        ),
    )(*args)


def solution(mesh):
    placed = (
        P("grp", "gy", "gz", None, None),
        P("grp", "gy", "gz", None),
        P("grp", "gy", "gz"),
        P("grp", "gy", "gz", None),
        P("grp", "gy", "gz", None),
        P("grp", "gy", "gz", None, None),
        P("grp", "gy", "gz", None),
        P("grp", "gy", "gz", None),
        P("grp", "gy", "gz", None),
        P("grp", "gy", "gz"),
        P("grp", "gy", "gz", None, None, None),
    )
    return jax.shard_map(
        functools.partial(local, mesh.shape["gy"], mesh.shape["gz"]),
        mesh=mesh,
        in_specs=placed,
        out_specs=P("grp", "gy", "gz", None),
        check_vma=False,
    )
```

```python
import functools
import math

import jax
import jax.numpy as jnp
from jax import lax
from jax.experimental import pallas as pl
from jax.experimental.pallas import tpu as pltpu
from jax.sharding import PartitionSpec as P

PB = 128
SLOTS = 9
ITERS = 3
KERNEL_WIDTH = 0.5
MESH = pl.DeviceIdType.MESH
KAPPA = math.sqrt(1.0 / (KERNEL_WIDTH * math.log(2.0)))
OFF = -1.0e4


def kernel(
    n_gy,
    n_gz,
    *refs,
):
    sources, out_ref, held, rest = refs[:11], refs[11], refs[12:23], refs[23:]
    off_ref, list_ref, cnt_ref, src_ref, p_ref, gc_ref = held[:6]
    sb_ref, st_ref, sg_ref, sc_ref, interp_ref = held[6:]
    (
        ext0,
        own8,
        pext,
        pden,
        wts,
        mask,
        first,
        later,
        got_first,
        got,
        buckets,
        got_buckets,
        onehot,
        num,
        den,
        h_send,
        h_recv,
        g_send,
        g_recv,
        r_send,
        r_recv,
        in_sem,
        known,
    ) = rest
    g = lax.axis_index("grp")
    y = lax.axis_index("gy")
    z = lax.axis_index("gz")
    rows_y, cols_z = off_ref.shape[1], off_ref.shape[3]
    n_near = n_gz // 2
    half, near = z // n_near, lax.rem(z, n_near)
    guards = gc_ref.shape[3]
    slots_out = sb_ref.shape[3]

    def at(gg, dy, dz):
        return (gg, lax.rem(y + dy + n_gy, n_gy), lax.rem(z + dz + n_gz, n_gz))

    stage1 = sorted(
        ((o, f) for o in range(n_gy) for f in range(2)),
        key=lambda of: -(min(of[0] // 2, (n_gy - of[0] + 1) // 2) + 0.1 * (of[0] % 2)),
    )
    stage2 = sorted(range(1, n_near), key=lambda o: -min(o, n_near - o))

    def at1(o, f):
        return (1 - g, y ^ o, (half ^ f) * n_near + near)

    def at2(o):
        return (g, y, half * n_near + (near ^ o))

    copies = [
        pltpu.make_async_copy(src, dst, in_sem.at[i])
        for i, (src, dst) in enumerate(zip(sources, held))
    ]
    copies[10].start()
    barrier = pltpu.get_barrier_semaphore()
    farthest = n_near // 2
    beside = [at(g, 1, 0), at(g, -1, 0)]
    beside += [
        (g, lax.rem(y + a + n_gy, n_gy), (half ^ 1) * n_near + near) for a in (-1, 0, 1)
    ]
    people = [at1(*of) for of in stage1] + [at2(o) for o in stage2 if o != farthest] + beside
    tellers = beside + [at2(1)]
    for who in people:
        pl.semaphore_signal(barrier, inc=1, device_id=who, device_id_type=MESH)
    for i in (4, 6, 0, 7, 8, 9, 1, 2, 3, 5):
        copies[i].start()

    sides = []
    for dy in (-1, 0, 1):
        for dz in (-1, 0, 1):
            if (dy, dz) == (0, 0):
                continue
            ys = {-1: (1, 1), 0: (1, rows_y), 1: (rows_y, 1)}[dy]
            zs = {-1: (1, 1), 0: (1, cols_z), 1: (cols_z, 1)}[dz]
            yd = {-1: rows_y + 1, 0: 1, 1: 0}[dy]
            zd = {-1: cols_z + 1, 0: 1, 1: 0}[dz]
            sides.append((dy, dz, ys, zs, yd, zd))

    def send_halo(buf, sem, which):
        for dy, dz, ys, zs, yd, zd in which:
            pltpu.make_async_remote_copy(
                src_ref=buf.at[pl.ds(ys[0], ys[1]), pl.ds(zs[0], zs[1])],
                dst_ref=buf.at[pl.ds(yd, ys[1]), pl.ds(zd, zs[1])],
                send_sem=h_send.at[sem],
                recv_sem=h_recv.at[sem],
                device_id=at(g, dy, dz),
                device_id_type=MESH,
            ).start()

    rows_sides = [s for s in sides if s[1] == 0]
    far_sides = [s for s in sides if s[1] != 0]

    def rim_wait(buf, sem, blocks):
        part = buf.at[pl.ds(0, blocks // cols_z), pl.ds(0, cols_z)]
        pltpu.make_async_copy(part, part, sem).wait()

    rows_rim = 2 * cols_z
    far_rim = 2 * rows_y + 4

    def send_values(src, dst, sweep):
        for o, f in stage1:
            pltpu.make_async_remote_copy(
                src_ref=src,
                dst_ref=dst.at[2 * o + f],
                send_sem=g_send.at[sweep],
                recv_sem=g_recv.at[sweep],
                device_id=at1(o, f),
                device_id_type=MESH,
            ).start()

    def send_buckets(sweep):
        for o in stage2:
            pltpu.make_async_remote_copy(
                src_ref=buckets.at[sweep, near ^ o],
                dst_ref=got_buckets.at[sweep, o - 1],
                send_sem=r_send.at[sweep],
                recv_sem=r_recv.at[sweep],
                device_id=at2(o),
                device_id_type=MESH,
            ).start()

    def whole_wait(ref, sem):
        pltpu.make_async_copy(ref, ref, sem).wait()

    row_id = lax.broadcasted_iota(jnp.int32, (PB, PB), 0)
    lane_id = lax.broadcasted_iota(jnp.int32, (PB, PB), 1)
    eye = row_id == lane_id

    def row_sums(acc):
        total = jnp.sum(acc, axis=1, keepdims=True)
        return jnp.sum(jnp.where(eye, total, 0.0), axis=0, keepdims=True)

    def interpolate(dst):
        for s in range(slots_out):
            press = pden[pl.ds(sb_ref[0, 0, 0, s], 1), :]
            dst[pl.ds(s, 1), :] = row_sums(interp_ref[0, 0, 0, s] * press)

    for i in (4, 6):
        copies[i].wait()
    for a in range(rows_y):
        pden[pl.ds(a * cols_z, cols_z), :] = p_ref[0, a]
    copies[10].wait()
    interpolate(first)
    for i in (7, 8, 9):
        copies[i].wait()
    codes = jnp.full((slots_out, PB), -1, jnp.int32)
    slot_row = lax.broadcasted_iota(jnp.int32, (slots_out, PB), 0)
    for s in range(slots_out):
        codes = jnp.where(slot_row == s, st_ref[0, 0, 0, s] * guards + sg_ref[0, 0, 0, s], codes)
    codes = jnp.where(slot_row < sc_ref[0, 0, 0], codes, -1)
    first[pl.ds(slots_out, slots_out), :] = codes.astype(jnp.float32)

    copies[0].wait()
    for a in range(rows_y):
        for k in range(3):
            scaled = (off_ref[0, a, k] - 0.5) * (2.0 * KAPPA)
            for b in range(cols_z):
                ext0[1 + a, 1 + b, pl.ds(k, 1), :] = scaled[b : b + 1]
                own8[a, b, pl.ds(k, 1), :] = 0.5 * scaled[b : b + 1]
        for b in range(cols_z):
            ext0[1 + a, 1 + b, pl.ds(3, 1), :] = p_ref[0, a, pl.ds(b, 1), :]

    pl.semaphore_wait(barrier, len(people))
    for who in tellers:
        pl.semaphore_signal(known, inc=1, device_id=who, device_id_type=MESH)
    send_values(first, got_first, 0)
    send_halo(ext0, ITERS, rows_sides)
    for i in (1, 2, 3, 5):
        copies[i].wait()

    for a in range(rows_y):
        lanes = lax.broadcasted_iota(jnp.int32, (cols_z, cols_z), 1)
        subs = lax.broadcasted_iota(jnp.int32, (cols_z, cols_z), 0)
        counts = jnp.sum(
            jnp.where(lanes == subs, cnt_ref[0, pl.ds(a, 1), :], 0).astype(jnp.float32),
            axis=1,
            keepdims=True,
        )
        places = lax.broadcasted_iota(jnp.int32, (cols_z, SLOTS), 1).astype(jnp.float32)
        for c in range(SLOTS):
            hit = (list_ref[0, a] == c) & (places < counts)
            active = jnp.sum(jnp.where(hit, 1.0, 0.0), axis=1, keepdims=True)
            mask[c, a] = jnp.broadcast_to((1.0 - active) * OFF, (cols_z, PB))

    def own_columns(a, b):
        cols = jnp.transpose(own8[a, b])
        cx = jnp.broadcast_to(cols[:, 0:1], (PB, PB))
        cy = jnp.broadcast_to(cols[:, 1:2], (PB, PB))
        cz = jnp.broadcast_to(cols[:, 2:3], (PB, PB))
        return cx, cy, cz, -(cx * cx + cy * cy + cz * cz)

    def make_weights(a, b, pairs):
        cx, cy, cz, cn = own_columns(a, b)
        for dy, dz in pairs:
            c = 3 * (dy + 1) + (dz + 1)
            near = ext0[1 + a + dy, 1 + b + dz]
            rx = near[0:1]
            ry = near[1:2] + 2.0 * KAPPA * dy
            rz = near[2:3] + 2.0 * KAPPA * dz
            rn = mask[c, a, pl.ds(b, 1), :] - 0.25 * (rx * rx + ry * ry + rz * rz)
            wts[a, b, c] = jnp.exp2((cn + rn) + (cx * rx + cy * ry) + cz * rz)

    all_dz = (-1, 0, 1)

    def inner(b, carry):
        for a in range(rows_y):
            dys = [dy for dy in (-1, 0, 1) if 0 <= a + dy < rows_y]
            make_weights(a, b, [(dy, dz) for dy in dys for dz in all_dz])
        return carry

    def outer(b, carry):
        for a in range(rows_y):
            dys = [dy for dy in (-1, 0, 1) if not 0 <= a + dy < rows_y]
            make_weights(a, b, [(dy, dz) for dy in dys for dz in all_dz])
        return carry

    def ends(far):
        for b, out in ((0, -1), (cols_z - 1, 1)):
            for a in range(rows_y):
                dzs = [dz for dz in all_dz if (dz == out) == far]
                make_weights(a, b, [(dy, dz) for dy in (-1, 0, 1) for dz in dzs])

    def deliver(values, sweep):
        hi = values.astype(jnp.bfloat16)
        rest = values - hi.astype(jnp.float32)
        mid = rest.astype(jnp.bfloat16)
        low = (rest - mid.astype(jnp.float32)).astype(jnp.bfloat16)
        sel = onehot[...]
        total = jnp.dot(sel, hi, preferred_element_type=jnp.float32)
        total += jnp.dot(sel, mid, preferred_element_type=jnp.float32)
        total += jnp.dot(sel, low, preferred_element_type=jnp.float32)
        buckets[sweep] = total.reshape(n_near, guards, PB)
        send_buckets(sweep)

    def sums(near_row, with_den, low, high):
        def body(b, carry):
            rows = [[near_row(e, b + k) for k in range(3)] for e in range(rows_y + 2)]
            for a in range(rows_y):
                acc = None
                tot = None
                for c in range(SLOTS):
                    w = wts[a, b, c]
                    part = w * rows[a + c // 3][c % 3]
                    acc = part if acc is None else acc + part
                    if with_den:
                        tot = w if tot is None else tot + w
                num[a, pl.ds(b, 1), :] = row_sums(acc)
                if with_den:
                    den[a, pl.ds(b, 1), :] = row_sums(tot)
            return carry

        lax.fori_loop(low, high, body, 0)

    lax.fori_loop(1, cols_z - 1, inner, 0)
    pl.semaphore_wait(known, len(tellers))
    send_halo(ext0, 0, far_sides)
    rim_wait(ext0, h_recv.at[ITERS], rows_rim)
    lax.fori_loop(1, cols_z - 1, outer, 0)
    ends(False)

    whole_wait(got_first, g_recv.at[0])
    entries = 2 * n_gy * slots_out
    dest = n_near * guards
    code_rows = got_first[:, pl.ds(slots_out, slots_out), :].reshape(entries, PB)[:, :dest]
    lane = lax.broadcasted_iota(jnp.int32, (entries, dest), 1)
    wanted = (y * n_gz + half * n_near) * guards + lane
    hits = jnp.where(code_rows == wanted.astype(jnp.float32), 1.0, 0.0)
    onehot[...] = jnp.transpose(hits).astype(jnp.bfloat16)
    deliver(got_first[:, pl.ds(0, slots_out), :].reshape(entries, PB), 0)

    def start_row(e, k):
        return ext0[e, k, pl.ds(3, 1), :]

    sums(start_row, True, 1, cols_z - 1)
    rim_wait(ext0, h_recv.at[0], far_rim)
    ends(True)
    sums(start_row, True, 0, 1)
    sums(start_row, True, cols_z - 1, cols_z)
    coef = gc_ref[0, 0, 0].reshape(rows_y, cols_z, PB)
    scale = 1.0 / (den[...] + coef + 1.0)

    for sweep in range(ITERS):
        base = num[...] - src_ref[0]
        whole_wait(got_buckets.at[sweep], r_recv.at[sweep])
        mine = buckets[sweep, near]
        for o in range(n_near - 1):
            mine = mine + got_buckets[sweep, o]
        new = (base + coef * mine.reshape(rows_y, cols_z, PB)) * scale
        if sweep == ITERS - 1:
            out_ref[0] = new
            break
        pden[...] = new.reshape(rows_y * cols_z, PB)
        interpolate(later.at[sweep])
        send_values(later.at[sweep], got.at[sweep], sweep + 1)
        press = pext.at[sweep]
        for a in range(rows_y):
            for b in range(cols_z):
                press[1 + a, 1 + b] = new[a, b : b + 1]
        send_halo(press, sweep + 1, sides)
        whole_wait(got.at[sweep], g_recv.at[sweep + 1])
        deliver(got[sweep].reshape(entries, PB), sweep + 1)
        rim_wait(press, h_recv.at[sweep + 1], rows_rim + far_rim)
        sums(lambda e, k: press[e, k], False, 0, cols_z)

    rim_wait(ext0, h_send.at[ITERS], rows_rim)
    rim_wait(ext0, h_send.at[0], far_rim)
    whole_wait(got_first, g_send.at[0])
    for sweep in range(ITERS):
        whole_wait(got_buckets.at[sweep], r_send.at[sweep])
        if sweep:
            rim_wait(pext.at[sweep - 1], h_send.at[sweep], rows_rim + far_rim)
            whole_wait(got.at[sweep - 1], g_send.at[sweep])


def local(n_gy, n_gz, *args):
    args = (jnp.swapaxes(args[0], 2, 3),) + args[1:]
    guard_coef, send_block = args[5], args[6]
    rows_y, cols_z = args[3].shape[1:3]
    guards = guard_coef.shape[3]
    slots_out = send_block.shape[3]
    n_near = n_gz // 2
    f32 = jnp.float32
    dma = pltpu.SemaphoreType.DMA((ITERS,))
    halo_dma = pltpu.SemaphoreType.DMA((ITERS + 1,))
    spaces = [pltpu.VMEM] * 6 + [pltpu.SMEM] * 4 + [pltpu.VMEM]
    return pl.pallas_call(
        functools.partial(kernel, n_gy, n_gz),
        out_shape=jax.ShapeDtypeStruct((1, rows_y, cols_z, PB), f32),
        in_specs=[pl.BlockSpec(memory_space=pl.ANY)] * len(args),
        out_specs=pl.BlockSpec(memory_space=pltpu.VMEM),
        scratch_shapes=[space(a.shape, a.dtype) for space, a in zip(spaces, args)]
        + [
            pltpu.VMEM((rows_y + 2, cols_z + 2, 4, PB), f32),
            pltpu.VMEM((rows_y, cols_z, 8, PB), f32),
            pltpu.VMEM((ITERS - 1, rows_y + 2, cols_z + 2, 1, PB), f32),
            pltpu.VMEM((rows_y * cols_z, PB), f32),
            pltpu.VMEM((rows_y, cols_z, SLOTS, PB, PB), f32),
            pltpu.VMEM((SLOTS, rows_y, cols_z, PB), f32),
            pltpu.VMEM((2 * slots_out, PB), f32),
            pltpu.VMEM((ITERS - 1, slots_out, PB), f32),
            pltpu.VMEM((2 * n_gy, 2 * slots_out, PB), f32),
            pltpu.VMEM((ITERS - 1, 2 * n_gy, slots_out, PB), f32),
            pltpu.VMEM((ITERS, n_near, guards, PB), f32),
            pltpu.VMEM((ITERS, n_near - 1, guards, PB), f32),
            pltpu.VMEM((n_near * guards, 2 * n_gy * slots_out), jnp.bfloat16),
            pltpu.VMEM((rows_y, cols_z, PB), f32),
            pltpu.VMEM((rows_y, cols_z, PB), f32),
            halo_dma,
            halo_dma,
            dma,
            dma,
            dma,
            dma,
            pltpu.SemaphoreType.DMA((len(args),)),
            pltpu.SemaphoreType.REGULAR,
        ],
        compiler_params=pltpu.CompilerParams(
            collective_id=0, has_side_effects=True, vmem_limit_bytes=60 * 1024 * 1024
        ),
    )(*args)


def solution(mesh):
    placed = (
        P("grp", "gy", "gz", None, None),
        P("grp", "gy", "gz", None),
        P("grp", "gy", "gz"),
        P("grp", "gy", "gz", None),
        P("grp", "gy", "gz", None),
        P("grp", "gy", "gz", None, None),
        P("grp", "gy", "gz", None),
        P("grp", "gy", "gz", None),
        P("grp", "gy", "gz", None),
        P("grp", "gy", "gz"),
        P("grp", "gy", "gz", None, None, None),
    )
    return jax.shard_map(
        functools.partial(local, mesh.shape["gy"], mesh.shape["gz"]),
        mesh=mesh,
        in_specs=placed,
        out_specs=P("grp", "gy", "gz", None),
        check_vma=False,
    )
```

```python
import functools
import math

import jax
import jax.numpy as jnp
from jax import lax
from jax.experimental import pallas as pl
from jax.experimental.pallas import tpu as pltpu
from jax.sharding import PartitionSpec as P

PB = 128
SLOTS = 9
ITERS = 3
KERNEL_WIDTH = 0.5
MESH = pl.DeviceIdType.MESH
KAPPA = math.sqrt(1.0 / (KERNEL_WIDTH * math.log(2.0)))
OFF = -1.0e4


def kernel(
    n_gy,
    n_gz,
    *refs,
):
    sources, out_ref, held, rest = refs[:11], refs[11], refs[12:23], refs[23:]
    off_ref, list_ref, cnt_ref, src_ref, p_ref, gc_ref = held[:6]
    sb_ref, st_ref, sg_ref, sc_ref, interp_ref = held[6:]
    (
        ext0,
        own8,
        pext,
        pden,
        wts,
        mask,
        first,
        later,
        got_first,
        got,
        buckets,
        got_buckets,
        onehot,
        num,
        den,
        h_send,
        h_recv,
        g_send,
        g_recv,
        r_send,
        r_recv,
        in_sem,
        known,
    ) = rest
    g = lax.axis_index("grp")
    y = lax.axis_index("gy")
    z = lax.axis_index("gz")
    rows_y, cols_z = off_ref.shape[1], off_ref.shape[3]
    n_near = n_gz // 2
    half, near = z // n_near, lax.rem(z, n_near)
    guards = gc_ref.shape[3]
    slots_out = sb_ref.shape[3]

    def at(gg, dy, dz):
        return (gg, lax.rem(y + dy + n_gy, n_gy), lax.rem(z + dz + n_gz, n_gz))

    stage1 = sorted(
        ((o, f) for o in range(n_gy) for f in range(2)),
        key=lambda of: -(min(of[0] // 2, (n_gy - of[0] + 1) // 2) + 0.1 * (of[0] % 2)),
    )
    stage2 = sorted(range(1, n_near), key=lambda o: -min(o, n_near - o))

    def at1(o, f):
        return (1 - g, y ^ o, (half ^ f) * n_near + near)

    def at2(o):
        return (g, y, half * n_near + (near ^ o))

    copies = [
        pltpu.make_async_copy(src, dst, in_sem.at[i])
        for i, (src, dst) in enumerate(zip(sources, held))
    ]
    copies[10].start()
    barrier = pltpu.get_barrier_semaphore()
    farthest = n_near // 2
    beside = [at(g, 1, 0), at(g, -1, 0)]
    beside += [
        (g, lax.rem(y + a + n_gy, n_gy), (half ^ 1) * n_near + near) for a in (-1, 0, 1)
    ]
    people = [at1(*of) for of in stage1] + [at2(o) for o in stage2 if o != farthest] + beside
    tellers = beside + [at2(1)]
    for who in people:
        pl.semaphore_signal(barrier, inc=1, device_id=who, device_id_type=MESH)
    for i in (4, 6, 0, 7, 8, 9, 1, 2, 3, 5):
        copies[i].start()

    sides = []
    for dy in (-1, 0, 1):
        for dz in (-1, 0, 1):
            if (dy, dz) == (0, 0):
                continue
            ys = {-1: (1, 1), 0: (1, rows_y), 1: (rows_y, 1)}[dy]
            zs = {-1: (1, 1), 0: (1, cols_z), 1: (cols_z, 1)}[dz]
            yd = {-1: rows_y + 1, 0: 1, 1: 0}[dy]
            zd = {-1: cols_z + 1, 0: 1, 1: 0}[dz]
            sides.append((dy, dz, ys, zs, yd, zd))

    def send_halo(buf, sem, which):
        for dy, dz, ys, zs, yd, zd in which:
            pltpu.make_async_remote_copy(
                src_ref=buf.at[pl.ds(ys[0], ys[1]), pl.ds(zs[0], zs[1])],
                dst_ref=buf.at[pl.ds(yd, ys[1]), pl.ds(zd, zs[1])],
                send_sem=h_send.at[sem],
                recv_sem=h_recv.at[sem],
                device_id=at(g, dy, dz),
                device_id_type=MESH,
            ).start()

    rows_sides = [s for s in sides if s[1] == 0]
    far_sides = [s for s in sides if s[1] != 0]

    def rim_wait(buf, sem, blocks):
        part = buf.at[pl.ds(0, blocks // cols_z), pl.ds(0, cols_z)]
        pltpu.make_async_copy(part, part, sem).wait()

    rows_rim = 2 * cols_z
    far_rim = 2 * rows_y + 4

    def send_values(src, dst, sweep):
        for o, f in stage1:
            pltpu.make_async_remote_copy(
                src_ref=src,
                dst_ref=dst.at[2 * o + f],
                send_sem=g_send.at[sweep],
                recv_sem=g_recv.at[sweep],
                device_id=at1(o, f),
                device_id_type=MESH,
            ).start()

    def send_buckets(sweep):
        for o in stage2:
            pltpu.make_async_remote_copy(
                src_ref=buckets.at[sweep, near ^ o],
                dst_ref=got_buckets.at[sweep, o - 1],
                send_sem=r_send.at[sweep],
                recv_sem=r_recv.at[sweep],
                device_id=at2(o),
                device_id_type=MESH,
            ).start()

    def whole_wait(ref, sem):
        pltpu.make_async_copy(ref, ref, sem).wait()

    row_id = lax.broadcasted_iota(jnp.int32, (PB, PB), 0)
    lane_id = lax.broadcasted_iota(jnp.int32, (PB, PB), 1)
    eye = row_id == lane_id

    def row_sums(acc):
        total = jnp.sum(acc, axis=1, keepdims=True)
        return jnp.sum(jnp.where(eye, total, 0.0), axis=0, keepdims=True)

    def interpolate(dst):
        for s in range(slots_out):
            press = pden[pl.ds(sb_ref[0, 0, 0, s], 1), :]
            dst[pl.ds(s, 1), :] = row_sums(interp_ref[0, 0, 0, s] * press)

    for i in (4, 6):
        copies[i].wait()
    for a in range(rows_y):
        pden[pl.ds(a * cols_z, cols_z), :] = p_ref[0, a]
    copies[10].wait()
    interpolate(first)
    for i in (7, 8, 9):
        copies[i].wait()
    codes = jnp.full((slots_out, PB), -1, jnp.int32)
    slot_row = lax.broadcasted_iota(jnp.int32, (slots_out, PB), 0)
    for s in range(slots_out):
        codes = jnp.where(slot_row == s, st_ref[0, 0, 0, s] * guards + sg_ref[0, 0, 0, s], codes)
    codes = jnp.where(slot_row < sc_ref[0, 0, 0], codes, -1)
    first[pl.ds(slots_out, slots_out), :] = codes.astype(jnp.float32)

    copies[0].wait()
    for a in range(rows_y):
        for k in range(3):
            scaled = (off_ref[0, a, k] - 0.5) * (2.0 * KAPPA)
            for b in range(cols_z):
                ext0[1 + a, 1 + b, pl.ds(k, 1), :] = scaled[b : b + 1]
                own8[a, b, pl.ds(k, 1), :] = 0.5 * scaled[b : b + 1]
        for b in range(cols_z):
            ext0[1 + a, 1 + b, pl.ds(3, 1), :] = p_ref[0, a, pl.ds(b, 1), :]

    pl.semaphore_wait(barrier, len(people))
    for who in tellers:
        pl.semaphore_signal(known, inc=1, device_id=who, device_id_type=MESH)
    send_values(first, got_first, 0)
    send_halo(ext0, ITERS, rows_sides)
    for i in (1, 2, 3, 5):
        copies[i].wait()

    for a in range(rows_y):
        lanes = lax.broadcasted_iota(jnp.int32, (cols_z, cols_z), 1)
        subs = lax.broadcasted_iota(jnp.int32, (cols_z, cols_z), 0)
        counts = jnp.sum(
            jnp.where(lanes == subs, cnt_ref[0, pl.ds(a, 1), :], 0).astype(jnp.float32),
            axis=1,
            keepdims=True,
        )
        places = lax.broadcasted_iota(jnp.int32, (cols_z, SLOTS), 1).astype(jnp.float32)
        for c in range(SLOTS):
            hit = (list_ref[0, a] == c) & (places < counts)
            active = jnp.sum(jnp.where(hit, 1.0, 0.0), axis=1, keepdims=True)
            mask[c, a] = jnp.broadcast_to((1.0 - active) * OFF, (cols_z, PB))

    def own_columns(a, b):
        cols = jnp.transpose(own8[a, b])
        cx = jnp.broadcast_to(cols[:, 0:1], (PB, PB))
        cy = jnp.broadcast_to(cols[:, 1:2], (PB, PB))
        cz = jnp.broadcast_to(cols[:, 2:3], (PB, PB))
        return cx, cy, cz, -(cx * cx + cy * cy + cz * cz)

    def make_weights(a, b, pairs):
        cx, cy, cz, cn = own_columns(a, b)
        for dy, dz in pairs:
            c = 3 * (dy + 1) + (dz + 1)
            near = ext0[1 + a + dy, 1 + b + dz]
            rx = near[0:1]
            ry = near[1:2] + 2.0 * KAPPA * dy
            rz = near[2:3] + 2.0 * KAPPA * dz
            rn = mask[c, a, pl.ds(b, 1), :] - 0.25 * (rx * rx + ry * ry + rz * rz)
            wts[a, b, c] = jnp.exp2((cn + rn) + (cx * rx + cy * ry) + cz * rz)

    all_dz = (-1, 0, 1)

    def inner(b, carry):
        for a in range(rows_y):
            dys = [dy for dy in (-1, 0, 1) if 0 <= a + dy < rows_y]
            make_weights(a, b, [(dy, dz) for dy in dys for dz in all_dz])
        return carry

    def outer(b, carry):
        for a in range(rows_y):
            dys = [dy for dy in (-1, 0, 1) if not 0 <= a + dy < rows_y]
            make_weights(a, b, [(dy, dz) for dy in dys for dz in all_dz])
        return carry

    def ends(far):
        for b, out in ((0, -1), (cols_z - 1, 1)):
            for a in range(rows_y):
                dzs = [dz for dz in all_dz if (dz == out) == far]
                make_weights(a, b, [(dy, dz) for dy in (-1, 0, 1) for dz in dzs])

    def deliver(values, sweep):
        hi = values.astype(jnp.bfloat16)
        rest = values - hi.astype(jnp.float32)
        mid = rest.astype(jnp.bfloat16)
        low = (rest - mid.astype(jnp.float32)).astype(jnp.bfloat16)
        sel = onehot[...]
        total = jnp.dot(sel, hi, preferred_element_type=jnp.float32)
        total += jnp.dot(sel, mid, preferred_element_type=jnp.float32)
        total += jnp.dot(sel, low, preferred_element_type=jnp.float32)
        buckets[sweep] = total.reshape(n_near, guards, PB)
        send_buckets(sweep)

    def sums(near_row, with_den, low, high):
        def body(b, carry):
            rows = [[near_row(e, b + k) for k in range(3)] for e in range(rows_y + 2)]
            for a in range(rows_y):
                acc = None
                tot = None
                for c in range(SLOTS):
                    w = wts[a, b, c]
                    part = w * rows[a + c // 3][c % 3]
                    acc = part if acc is None else acc + part
                    if with_den:
                        tot = w if tot is None else tot + w
                num[a, pl.ds(b, 1), :] = row_sums(acc)
                if with_den:
                    den[a, pl.ds(b, 1), :] = row_sums(tot)
            return carry

        lax.fori_loop(low, high, body, 0)

    lax.fori_loop(1, cols_z - 1, inner, 0)
    pl.semaphore_wait(known, len(tellers))
    send_halo(ext0, 0, far_sides)
    whole_wait(got_first, g_recv.at[0])
    entries = 2 * n_gy * slots_out
    dest = n_near * guards
    code_rows = got_first[:, pl.ds(slots_out, slots_out), :].reshape(entries, PB)[:, :dest]
    lane = lax.broadcasted_iota(jnp.int32, (entries, dest), 1)
    wanted = (y * n_gz + half * n_near) * guards + lane
    hits = jnp.where(code_rows == wanted.astype(jnp.float32), 1.0, 0.0)
    onehot[...] = jnp.transpose(hits).astype(jnp.bfloat16)
    deliver(got_first[:, pl.ds(0, slots_out), :].reshape(entries, PB), 0)

    rim_wait(ext0, h_recv.at[ITERS], rows_rim)
    lax.fori_loop(1, cols_z - 1, outer, 0)
    ends(False)

    def start_row(e, k):
        return ext0[e, k, pl.ds(3, 1), :]

    sums(start_row, True, 1, cols_z - 1)
    rim_wait(ext0, h_recv.at[0], far_rim)
    ends(True)
    sums(start_row, True, 0, 1)
    sums(start_row, True, cols_z - 1, cols_z)
    coef = gc_ref[0, 0, 0].reshape(rows_y, cols_z, PB)
    scale = 1.0 / (den[...] + coef + 1.0)

    for sweep in range(ITERS):
        base = num[...] - src_ref[0]
        whole_wait(got_buckets.at[sweep], r_recv.at[sweep])
        mine = buckets[sweep, near]
        for o in range(n_near - 1):
            mine = mine + got_buckets[sweep, o]
        new = (base + coef * mine.reshape(rows_y, cols_z, PB)) * scale
        if sweep == ITERS - 1:
            out_ref[0] = new
            break
        pden[...] = new.reshape(rows_y * cols_z, PB)
        interpolate(later.at[sweep])
        send_values(later.at[sweep], got.at[sweep], sweep + 1)
        press = pext.at[sweep]
        for a in range(rows_y):
            for b in range(cols_z):
                press[1 + a, 1 + b] = new[a, b : b + 1]
        send_halo(press, sweep + 1, sides)
        whole_wait(got.at[sweep], g_recv.at[sweep + 1])
        deliver(got[sweep].reshape(entries, PB), sweep + 1)
        rim_wait(press, h_recv.at[sweep + 1], rows_rim + far_rim)
        sums(lambda e, k: press[e, k], False, 0, cols_z)

    rim_wait(ext0, h_send.at[ITERS], rows_rim)
    rim_wait(ext0, h_send.at[0], far_rim)
    whole_wait(got_first, g_send.at[0])
    for sweep in range(ITERS):
        whole_wait(got_buckets.at[sweep], r_send.at[sweep])
        if sweep:
            rim_wait(pext.at[sweep - 1], h_send.at[sweep], rows_rim + far_rim)
            whole_wait(got.at[sweep - 1], g_send.at[sweep])


def local(n_gy, n_gz, *args):
    args = (jnp.swapaxes(args[0], 2, 3),) + args[1:]
    guard_coef, send_block = args[5], args[6]
    rows_y, cols_z = args[3].shape[1:3]
    guards = guard_coef.shape[3]
    slots_out = send_block.shape[3]
    n_near = n_gz // 2
    f32 = jnp.float32
    dma = pltpu.SemaphoreType.DMA((ITERS,))
    halo_dma = pltpu.SemaphoreType.DMA((ITERS + 1,))
    spaces = [pltpu.VMEM] * 6 + [pltpu.SMEM] * 4 + [pltpu.VMEM]
    return pl.pallas_call(
        functools.partial(kernel, n_gy, n_gz),
        out_shape=pltpu.VMEM((1, rows_y, cols_z, PB), f32),
        in_specs=[pl.BlockSpec(memory_space=pl.ANY)] * len(args),
        out_specs=pl.BlockSpec(memory_space=pltpu.VMEM),
        scratch_shapes=[space(a.shape, a.dtype) for space, a in zip(spaces, args)]
        + [
            pltpu.VMEM((rows_y + 2, cols_z + 2, 4, PB), f32),
            pltpu.VMEM((rows_y, cols_z, 8, PB), f32),
            pltpu.VMEM((ITERS - 1, rows_y + 2, cols_z + 2, 1, PB), f32),
            pltpu.VMEM((rows_y * cols_z, PB), f32),
            pltpu.VMEM((rows_y, cols_z, SLOTS, PB, PB), f32),
            pltpu.VMEM((SLOTS, rows_y, cols_z, PB), f32),
            pltpu.VMEM((2 * slots_out, PB), f32),
            pltpu.VMEM((ITERS - 1, slots_out, PB), f32),
            pltpu.VMEM((2 * n_gy, 2 * slots_out, PB), f32),
            pltpu.VMEM((ITERS - 1, 2 * n_gy, slots_out, PB), f32),
            pltpu.VMEM((ITERS, n_near, guards, PB), f32),
            pltpu.VMEM((ITERS, n_near - 1, guards, PB), f32),
            pltpu.VMEM((n_near * guards, 2 * n_gy * slots_out), jnp.bfloat16),
            pltpu.VMEM((rows_y, cols_z, PB), f32),
            pltpu.VMEM((rows_y, cols_z, PB), f32),
            halo_dma,
            halo_dma,
            dma,
            dma,
            dma,
            dma,
            pltpu.SemaphoreType.DMA((len(args),)),
            pltpu.SemaphoreType.REGULAR,
        ],
        compiler_params=pltpu.CompilerParams(
            collective_id=0, has_side_effects=True, vmem_limit_bytes=60 * 1024 * 1024
        ),
    )(*args)


def solution(mesh):
    placed = (
        P("grp", "gy", "gz", None, None),
        P("grp", "gy", "gz", None),
        P("grp", "gy", "gz"),
        P("grp", "gy", "gz", None),
        P("grp", "gy", "gz", None),
        P("grp", "gy", "gz", None, None),
        P("grp", "gy", "gz", None),
        P("grp", "gy", "gz", None),
        P("grp", "gy", "gz", None),
        P("grp", "gy", "gz"),
        P("grp", "gy", "gz", None, None, None),
    )
    return jax.shard_map(
        functools.partial(local, mesh.shape["gy"], mesh.shape["gz"]),
        mesh=mesh,
        in_specs=placed,
        out_specs=P("grp", "gy", "gz", None),
        check_vma=False,
    )
```

```python
import functools
import math

import jax
import jax.numpy as jnp
from jax import lax
from jax.experimental import pallas as pl
from jax.experimental.pallas import tpu as pltpu
from jax.sharding import PartitionSpec as P

PB = 128
SLOTS = 9
ITERS = 3
KERNEL_WIDTH = 0.5
MESH = pl.DeviceIdType.MESH
KAPPA = math.sqrt(1.0 / (KERNEL_WIDTH * math.log(2.0)))
OFF = -1.0e4


def kernel(
    n_gy,
    n_gz,
    *refs,
):
    sources, out_ref, held, rest = refs[:11], refs[11], refs[12:23], refs[23:]
    off_ref, list_ref, cnt_ref, src_ref, p_ref, gc_ref = held[:6]
    sb_ref, st_ref, sg_ref, sc_ref, interp_ref = held[6:]
    (
        ext0,
        own8,
        pext,
        pden,
        wts,
        mask,
        first,
        later,
        got_first,
        got,
        buckets,
        got_buckets,
        onehot,
        num,
        den,
        h_send,
        h_recv,
        g_send,
        g_recv,
        r_send,
        r_recv,
        in_sem,
        known,
    ) = rest
    g = lax.axis_index("grp")
    y = lax.axis_index("gy")
    z = lax.axis_index("gz")
    rows_y, cols_z = off_ref.shape[1], off_ref.shape[3]
    n_near = n_gz // 2
    half, near = z // n_near, lax.rem(z, n_near)
    guards = gc_ref.shape[3]
    slots_out = sb_ref.shape[3]

    def at(gg, dy, dz):
        return (gg, lax.rem(y + dy + n_gy, n_gy), lax.rem(z + dz + n_gz, n_gz))

    stage1 = sorted(
        ((o, f) for o in range(n_gy) for f in range(2)),
        key=lambda of: -(min(of[0] // 2, (n_gy - of[0] + 1) // 2) + 0.1 * (of[0] % 2)),
    )
    stage2 = sorted(range(1, n_near), key=lambda o: -min(o, n_near - o))

    def at1(o, f):
        return (1 - g, y ^ o, (half ^ f) * n_near + near)

    def at2(o):
        return (g, y, half * n_near + (near ^ o))

    copies = [
        pltpu.make_async_copy(src, dst, in_sem.at[i])
        for i, (src, dst) in enumerate(zip(sources, held))
    ]
    for i in (4, 6, 10):
        copies[i].start()
    barrier = pltpu.get_barrier_semaphore()
    farthest = n_near // 2
    beside = [at(g, 1, 0), at(g, -1, 0)]
    beside += [
        (g, lax.rem(y + a + n_gy, n_gy), (half ^ 1) * n_near + near) for a in (-1, 0, 1)
    ]
    people = [at1(*of) for of in stage1] + [at2(o) for o in stage2 if o != farthest] + beside
    tellers = beside + [at2(1)]
    for who in people:
        pl.semaphore_signal(barrier, inc=1, device_id=who, device_id_type=MESH)
    for i in (7, 8, 9, 0, 1, 2, 3, 5):
        copies[i].start()

    sides = []
    for dy in (-1, 0, 1):
        for dz in (-1, 0, 1):
            if (dy, dz) == (0, 0):
                continue
            ys = {-1: (1, 1), 0: (1, rows_y), 1: (rows_y, 1)}[dy]
            zs = {-1: (1, 1), 0: (1, cols_z), 1: (cols_z, 1)}[dz]
            yd = {-1: rows_y + 1, 0: 1, 1: 0}[dy]
            zd = {-1: cols_z + 1, 0: 1, 1: 0}[dz]
            sides.append((dy, dz, ys, zs, yd, zd))

    def send_halo(buf, sem, which):
        for dy, dz, ys, zs, yd, zd in which:
            pltpu.make_async_remote_copy(
                src_ref=buf.at[pl.ds(ys[0], ys[1]), pl.ds(zs[0], zs[1])],
                dst_ref=buf.at[pl.ds(yd, ys[1]), pl.ds(zd, zs[1])],
                send_sem=h_send.at[sem],
                recv_sem=h_recv.at[sem],
                device_id=at(g, dy, dz),
                device_id_type=MESH,
            ).start()

    rows_sides = [s for s in sides if s[1] == 0]
    far_sides = [s for s in sides if s[1] != 0]

    def rim_wait(buf, sem, blocks):
        part = buf.at[pl.ds(0, blocks // cols_z), pl.ds(0, cols_z)]
        pltpu.make_async_copy(part, part, sem).wait()

    rows_rim = 2 * cols_z
    far_rim = 2 * rows_y + 4

    def send_values(src, dst, sweep):
        for o, f in stage1:
            pltpu.make_async_remote_copy(
                src_ref=src,
                dst_ref=dst.at[2 * o + f],
                send_sem=g_send.at[sweep],
                recv_sem=g_recv.at[sweep],
                device_id=at1(o, f),
                device_id_type=MESH,
            ).start()

    def send_buckets(sweep):
        for o in stage2:
            pltpu.make_async_remote_copy(
                src_ref=buckets.at[sweep, near ^ o],
                dst_ref=got_buckets.at[sweep, o - 1],
                send_sem=r_send.at[sweep],
                recv_sem=r_recv.at[sweep],
                device_id=at2(o),
                device_id_type=MESH,
            ).start()

    def whole_wait(ref, sem):
        pltpu.make_async_copy(ref, ref, sem).wait()

    row_id = lax.broadcasted_iota(jnp.int32, (PB, PB), 0)
    lane_id = lax.broadcasted_iota(jnp.int32, (PB, PB), 1)
    eye = row_id == lane_id

    def row_sums(acc):
        total = jnp.sum(acc, axis=1, keepdims=True)
        return jnp.sum(jnp.where(eye, total, 0.0), axis=0, keepdims=True)

    def interpolate(dst):
        for s in range(slots_out):
            press = pden[pl.ds(sb_ref[0, 0, 0, s], 1), :]
            dst[pl.ds(s, 1), :] = row_sums(interp_ref[0, 0, 0, s] * press)

    for i in (4, 6):
        copies[i].wait()
    for a in range(rows_y):
        pden[pl.ds(a * cols_z, cols_z), :] = p_ref[0, a]
    copies[10].wait()
    interpolate(first)
    for i in (7, 8, 9):
        copies[i].wait()
    codes = jnp.full((slots_out, PB), -1, jnp.int32)
    slot_row = lax.broadcasted_iota(jnp.int32, (slots_out, PB), 0)
    for s in range(slots_out):
        codes = jnp.where(slot_row == s, st_ref[0, 0, 0, s] * guards + sg_ref[0, 0, 0, s], codes)
    codes = jnp.where(slot_row < sc_ref[0, 0, 0], codes, -1)
    first[pl.ds(slots_out, slots_out), :] = codes.astype(jnp.float32)

    pl.semaphore_wait(barrier, len(people))
    for who in tellers:
        pl.semaphore_signal(known, inc=1, device_id=who, device_id_type=MESH)
    send_values(first, got_first, 0)

    copies[0].wait()
    for a in range(rows_y):
        for k in range(3):
            scaled = (off_ref[0, a, k] - 0.5) * (2.0 * KAPPA)
            for b in range(cols_z):
                ext0[1 + a, 1 + b, pl.ds(k, 1), :] = scaled[b : b + 1]
                own8[a, b, pl.ds(k, 1), :] = 0.5 * scaled[b : b + 1]
        for b in range(cols_z):
            ext0[1 + a, 1 + b, pl.ds(3, 1), :] = p_ref[0, a, pl.ds(b, 1), :]
    send_halo(ext0, ITERS, rows_sides)
    for i in (1, 2, 3, 5):
        copies[i].wait()

    for a in range(rows_y):
        lanes = lax.broadcasted_iota(jnp.int32, (cols_z, cols_z), 1)
        subs = lax.broadcasted_iota(jnp.int32, (cols_z, cols_z), 0)
        counts = jnp.sum(
            jnp.where(lanes == subs, cnt_ref[0, pl.ds(a, 1), :], 0).astype(jnp.float32),
            axis=1,
            keepdims=True,
        )
        places = lax.broadcasted_iota(jnp.int32, (cols_z, SLOTS), 1).astype(jnp.float32)
        for c in range(SLOTS):
            hit = (list_ref[0, a] == c) & (places < counts)
            active = jnp.sum(jnp.where(hit, 1.0, 0.0), axis=1, keepdims=True)
            mask[c, a] = jnp.broadcast_to((1.0 - active) * OFF, (cols_z, PB))

    def own_columns(a, b):
        cols = jnp.transpose(own8[a, b])
        cx = jnp.broadcast_to(cols[:, 0:1], (PB, PB))
        cy = jnp.broadcast_to(cols[:, 1:2], (PB, PB))
        cz = jnp.broadcast_to(cols[:, 2:3], (PB, PB))
        return cx, cy, cz, -(cx * cx + cy * cy + cz * cz)

    def make_weights(a, b, pairs):
        cx, cy, cz, cn = own_columns(a, b)
        for dy, dz in pairs:
            c = 3 * (dy + 1) + (dz + 1)
            near = ext0[1 + a + dy, 1 + b + dz]
            rx = near[0:1]
            ry = near[1:2] + 2.0 * KAPPA * dy
            rz = near[2:3] + 2.0 * KAPPA * dz
            rn = mask[c, a, pl.ds(b, 1), :] - 0.25 * (rx * rx + ry * ry + rz * rz)
            wts[a, b, c] = jnp.exp2((cn + rn) + (cx * rx + cy * ry) + cz * rz)

    all_dz = (-1, 0, 1)

    def inner(b, carry):
        for a in range(rows_y):
            dys = [dy for dy in (-1, 0, 1) if 0 <= a + dy < rows_y]
            make_weights(a, b, [(dy, dz) for dy in dys for dz in all_dz])
        return carry

    def outer(b, carry):
        for a in range(rows_y):
            dys = [dy for dy in (-1, 0, 1) if not 0 <= a + dy < rows_y]
            make_weights(a, b, [(dy, dz) for dy in dys for dz in all_dz])
        return carry

    def ends(far):
        for b, out in ((0, -1), (cols_z - 1, 1)):
            for a in range(rows_y):
                dzs = [dz for dz in all_dz if (dz == out) == far]
                make_weights(a, b, [(dy, dz) for dy in (-1, 0, 1) for dz in dzs])

    def deliver(values, sweep):
        hi = values.astype(jnp.bfloat16)
        rest = values - hi.astype(jnp.float32)
        mid = rest.astype(jnp.bfloat16)
        low = (rest - mid.astype(jnp.float32)).astype(jnp.bfloat16)
        sel = onehot[...]
        total = jnp.dot(sel, hi, preferred_element_type=jnp.float32)
        total += jnp.dot(sel, mid, preferred_element_type=jnp.float32)
        total += jnp.dot(sel, low, preferred_element_type=jnp.float32)
        buckets[sweep] = total.reshape(n_near, guards, PB)
        send_buckets(sweep)

    def sums(near_row, with_den, low, high):
        def body(b, carry):
            rows = [[near_row(e, b + k) for k in range(3)] for e in range(rows_y + 2)]
            for a in range(rows_y):
                acc = None
                tot = None
                for c in range(SLOTS):
                    w = wts[a, b, c]
                    part = w * rows[a + c // 3][c % 3]
                    acc = part if acc is None else acc + part
                    if with_den:
                        tot = w if tot is None else tot + w
                num[a, pl.ds(b, 1), :] = row_sums(acc)
                if with_den:
                    den[a, pl.ds(b, 1), :] = row_sums(tot)
            return carry

        lax.fori_loop(low, high, body, 0)

    lax.fori_loop(1, cols_z - 1, inner, 0)
    pl.semaphore_wait(known, len(tellers))
    send_halo(ext0, 0, far_sides)
    rim_wait(ext0, h_recv.at[ITERS], rows_rim)
    middle = cols_z // 2
    lax.fori_loop(1, middle, outer, 0)
    whole_wait(got_first, g_recv.at[0])
    entries = 2 * n_gy * slots_out
    dest = n_near * guards
    code_rows = got_first[:, pl.ds(slots_out, slots_out), :].reshape(entries, PB)[:, :dest]
    lane = lax.broadcasted_iota(jnp.int32, (entries, dest), 1)
    wanted = (y * n_gz + half * n_near) * guards + lane
    hits = jnp.where(code_rows == wanted.astype(jnp.float32), 1.0, 0.0)
    onehot[...] = jnp.transpose(hits).astype(jnp.bfloat16)
    deliver(got_first[:, pl.ds(0, slots_out), :].reshape(entries, PB), 0)

    lax.fori_loop(middle, cols_z - 1, outer, 0)
    ends(False)

    def start_row(e, k):
        return ext0[e, k, pl.ds(3, 1), :]

    sums(start_row, True, 1, cols_z - 1)
    rim_wait(ext0, h_recv.at[0], far_rim)
    ends(True)
    sums(start_row, True, 0, 1)
    sums(start_row, True, cols_z - 1, cols_z)
    coef = gc_ref[0, 0, 0].reshape(rows_y, cols_z, PB)
    scale = 1.0 / (den[...] + coef + 1.0)

    for sweep in range(ITERS):
        base = num[...] - src_ref[0]
        whole_wait(got_buckets.at[sweep], r_recv.at[sweep])
        mine = buckets[sweep, near]
        for o in range(n_near - 1):
            mine = mine + got_buckets[sweep, o]
        new = (base + coef * mine.reshape(rows_y, cols_z, PB)) * scale
        if sweep == ITERS - 1:
            out_ref[0] = new
            break
        pden[...] = new.reshape(rows_y * cols_z, PB)
        interpolate(later.at[sweep])
        send_values(later.at[sweep], got.at[sweep], sweep + 1)
        press = pext.at[sweep]
        for a in range(rows_y):
            for b in range(cols_z):
                press[1 + a, 1 + b] = new[a, b : b + 1]
        send_halo(press, sweep + 1, sides)
        whole_wait(got.at[sweep], g_recv.at[sweep + 1])
        deliver(got[sweep].reshape(entries, PB), sweep + 1)
        rim_wait(press, h_recv.at[sweep + 1], rows_rim + far_rim)
        sums(lambda e, k: press[e, k], False, 0, cols_z)

    rim_wait(ext0, h_send.at[ITERS], rows_rim)
    rim_wait(ext0, h_send.at[0], far_rim)
    whole_wait(got_first, g_send.at[0])
    for sweep in range(ITERS):
        whole_wait(got_buckets.at[sweep], r_send.at[sweep])
        if sweep:
            rim_wait(pext.at[sweep - 1], h_send.at[sweep], rows_rim + far_rim)
            whole_wait(got.at[sweep - 1], g_send.at[sweep])


def local(n_gy, n_gz, *args):
    args = (jnp.swapaxes(args[0], 2, 3),) + args[1:]
    guard_coef, send_block = args[5], args[6]
    rows_y, cols_z = args[3].shape[1:3]
    guards = guard_coef.shape[3]
    slots_out = send_block.shape[3]
    n_near = n_gz // 2
    f32 = jnp.float32
    dma = pltpu.SemaphoreType.DMA((ITERS,))
    halo_dma = pltpu.SemaphoreType.DMA((ITERS + 1,))
    spaces = [pltpu.VMEM] * 6 + [pltpu.SMEM] * 4 + [pltpu.VMEM]
    return pl.pallas_call(
        functools.partial(kernel, n_gy, n_gz),
        out_shape=pltpu.VMEM((1, rows_y, cols_z, PB), f32),
        in_specs=[pl.BlockSpec(memory_space=pl.ANY)] * len(args),
        out_specs=pl.BlockSpec(memory_space=pltpu.VMEM),
        scratch_shapes=[space(a.shape, a.dtype) for space, a in zip(spaces, args)]
        + [
            pltpu.VMEM((rows_y + 2, cols_z + 2, 4, PB), f32),
            pltpu.VMEM((rows_y, cols_z, 8, PB), f32),
            pltpu.VMEM((ITERS - 1, rows_y + 2, cols_z + 2, 1, PB), f32),
            pltpu.VMEM((rows_y * cols_z, PB), f32),
            pltpu.VMEM((rows_y, cols_z, SLOTS, PB, PB), f32),
            pltpu.VMEM((SLOTS, rows_y, cols_z, PB), f32),
            pltpu.VMEM((2 * slots_out, PB), f32),
            pltpu.VMEM((ITERS - 1, slots_out, PB), f32),
            pltpu.VMEM((2 * n_gy, 2 * slots_out, PB), f32),
            pltpu.VMEM((ITERS - 1, 2 * n_gy, slots_out, PB), f32),
            pltpu.VMEM((ITERS, n_near, guards, PB), f32),
            pltpu.VMEM((ITERS, n_near - 1, guards, PB), f32),
            pltpu.VMEM((n_near * guards, 2 * n_gy * slots_out), jnp.bfloat16),
            pltpu.VMEM((rows_y, cols_z, PB), f32),
            pltpu.VMEM((rows_y, cols_z, PB), f32),
            halo_dma,
            halo_dma,
            dma,
            dma,
            dma,
            dma,
            pltpu.SemaphoreType.DMA((len(args),)),
            pltpu.SemaphoreType.REGULAR,
        ],
        compiler_params=pltpu.CompilerParams(
            collective_id=0, has_side_effects=True, vmem_limit_bytes=60 * 1024 * 1024
        ),
    )(*args)


def solution(mesh):
    placed = (
        P("grp", "gy", "gz", None, None),
        P("grp", "gy", "gz", None),
        P("grp", "gy", "gz"),
        P("grp", "gy", "gz", None),
        P("grp", "gy", "gz", None),
        P("grp", "gy", "gz", None, None),
        P("grp", "gy", "gz", None),
        P("grp", "gy", "gz", None),
        P("grp", "gy", "gz", None),
        P("grp", "gy", "gz"),
        P("grp", "gy", "gz", None, None, None),
    )
    return jax.shard_map(
        functools.partial(local, mesh.shape["gy"], mesh.shape["gz"]),
        mesh=mesh,
        in_specs=placed,
        out_specs=P("grp", "gy", "gz", None),
        check_vma=False,
    )
```

```python
import functools
import math

import jax
import jax.numpy as jnp
from jax import lax
from jax.experimental import pallas as pl
from jax.experimental.pallas import tpu as pltpu
from jax.sharding import PartitionSpec as P

PB = 128
SLOTS = 9
ITERS = 3
KERNEL_WIDTH = 0.5
MESH = pl.DeviceIdType.MESH
KAPPA = math.sqrt(1.0 / (KERNEL_WIDTH * math.log(2.0)))
OFF = -1.0e4


def kernel(
    n_gy,
    n_gz,
    *refs,
):
    sources, out_ref, held, rest = refs[:11], refs[11], refs[12:23], refs[23:]
    off_ref, list_ref, cnt_ref, src_ref, p_ref, gc_ref = held[:6]
    sb_ref, st_ref, sg_ref, sc_ref, interp_ref = held[6:]
    (
        ext0,
        own8,
        pext,
        pden,
        wts,
        mask,
        first,
        later,
        got_first,
        got,
        buckets,
        got_buckets,
        onehot,
        num,
        den,
        h_send,
        h_recv,
        g_send,
        g_recv,
        r_send,
        r_recv,
        in_sem,
        known,
    ) = rest
    g = lax.axis_index("grp")
    y = lax.axis_index("gy")
    z = lax.axis_index("gz")
    rows_y, cols_z = off_ref.shape[1], off_ref.shape[3]
    n_near = n_gz // 2
    half, near = z // n_near, lax.rem(z, n_near)
    guards = gc_ref.shape[3]
    slots_out = sb_ref.shape[3]

    def at(gg, dy, dz):
        return (gg, lax.rem(y + dy + n_gy, n_gy), lax.rem(z + dz + n_gz, n_gz))

    across = [o for o in (4, 5, 6, 7, 2, 3, 1, 0) if o < n_gy]
    stage1 = [(o, 1) for o in across[:6]] + [(o, 0) for o in across[:4]]
    stage1 += [(o, 1) for o in across[6:]] + [(o, 0) for o in across[4:]]
    stage2 = [o for o in (4, 5, 7, 6, 3, 2, 1) if o < n_near]

    def at1(o, f):
        return (1 - g, y ^ o, (half ^ f) * n_near + near)

    def at2(o):
        return (g, y, half * n_near + (near ^ o))

    copies = [
        pltpu.make_async_copy(src, dst, in_sem.at[i])
        for i, (src, dst) in enumerate(zip(sources, held))
    ]
    for i in (4, 6, 10):
        copies[i].start()
    barrier = pltpu.get_barrier_semaphore()
    farthest = n_near // 2
    beside = [at(g, 1, 0), at(g, -1, 0)]
    beside += [
        (g, lax.rem(y + a + n_gy, n_gy), (half ^ 1) * n_near + near) for a in (-1, 0, 1)
    ]
    people = [at1(*of) for of in stage1] + [at2(o) for o in stage2 if o != farthest] + beside
    tellers = beside + [at2(1)]
    for who in people:
        pl.semaphore_signal(barrier, inc=1, device_id=who, device_id_type=MESH)
    for i in (7, 8, 9, 0, 1, 2, 3, 5):
        copies[i].start()

    sides = []
    for dy in (-1, 0, 1):
        for dz in (-1, 0, 1):
            if (dy, dz) == (0, 0):
                continue
            ys = {-1: (1, 1), 0: (1, rows_y), 1: (rows_y, 1)}[dy]
            zs = {-1: (1, 1), 0: (1, cols_z), 1: (cols_z, 1)}[dz]
            yd = {-1: rows_y + 1, 0: 1, 1: 0}[dy]
            zd = {-1: cols_z + 1, 0: 1, 1: 0}[dz]
            sides.append((dy, dz, ys, zs, yd, zd))

    def send_halo(buf, sem, which):
        for dy, dz, ys, zs, yd, zd in which:
            pltpu.make_async_remote_copy(
                src_ref=buf.at[pl.ds(ys[0], ys[1]), pl.ds(zs[0], zs[1])],
                dst_ref=buf.at[pl.ds(yd, ys[1]), pl.ds(zd, zs[1])],
                send_sem=h_send.at[sem],
                recv_sem=h_recv.at[sem],
                device_id=at(g, dy, dz),
                device_id_type=MESH,
            ).start()

    rows_sides = [s for s in sides if s[1] == 0]
    far_sides = [s for s in sides if s[1] != 0]

    def rim_wait(buf, sem, blocks):
        part = buf.at[pl.ds(0, blocks // cols_z), pl.ds(0, cols_z)]
        pltpu.make_async_copy(part, part, sem).wait()

    rows_rim = 2 * cols_z
    far_rim = 2 * rows_y + 4

    def send_values(src, dst, sweep):
        for o, f in stage1:
            pltpu.make_async_remote_copy(
                src_ref=src,
                dst_ref=dst.at[2 * o + f],
                send_sem=g_send.at[sweep],
                recv_sem=g_recv.at[sweep],
                device_id=at1(o, f),
                device_id_type=MESH,
            ).start()

    def send_buckets(sweep):
        for o in stage2:
            pltpu.make_async_remote_copy(
                src_ref=buckets.at[sweep, near ^ o],
                dst_ref=got_buckets.at[sweep, o - 1],
                send_sem=r_send.at[sweep],
                recv_sem=r_recv.at[sweep],
                device_id=at2(o),
                device_id_type=MESH,
            ).start()

    def whole_wait(ref, sem):
        pltpu.make_async_copy(ref, ref, sem).wait()

    row_id = lax.broadcasted_iota(jnp.int32, (PB, PB), 0)
    lane_id = lax.broadcasted_iota(jnp.int32, (PB, PB), 1)
    eye = row_id == lane_id

    def row_sums(acc):
        total = jnp.sum(acc, axis=1, keepdims=True)
        return jnp.sum(jnp.where(eye, total, 0.0), axis=0, keepdims=True)

    def interpolate(dst):
        for s in range(slots_out):
            press = pden[pl.ds(sb_ref[0, 0, 0, s], 1), :]
            dst[pl.ds(s, 1), :] = row_sums(interp_ref[0, 0, 0, s] * press)

    for i in (4, 6):
        copies[i].wait()
    for a in range(rows_y):
        pden[pl.ds(a * cols_z, cols_z), :] = p_ref[0, a]
    copies[10].wait()
    interpolate(first)
    for i in (7, 8, 9):
        copies[i].wait()
    codes = jnp.full((slots_out, PB), -1, jnp.int32)
    slot_row = lax.broadcasted_iota(jnp.int32, (slots_out, PB), 0)
    for s in range(slots_out):
        codes = jnp.where(slot_row == s, st_ref[0, 0, 0, s] * guards + sg_ref[0, 0, 0, s], codes)
    codes = jnp.where(slot_row < sc_ref[0, 0, 0], codes, -1)
    first[pl.ds(slots_out, slots_out), :] = codes.astype(jnp.float32)

    pl.semaphore_wait(barrier, len(people))
    for who in tellers:
        pl.semaphore_signal(known, inc=1, device_id=who, device_id_type=MESH)
    send_values(first, got_first, 0)

    copies[0].wait()
    for a in range(rows_y):
        for k in range(3):
            scaled = (off_ref[0, a, k] - 0.5) * (2.0 * KAPPA)
            for b in range(cols_z):
                ext0[1 + a, 1 + b, pl.ds(k, 1), :] = scaled[b : b + 1]
                own8[a, b, pl.ds(k, 1), :] = 0.5 * scaled[b : b + 1]
        for b in range(cols_z):
            ext0[1 + a, 1 + b, pl.ds(3, 1), :] = p_ref[0, a, pl.ds(b, 1), :]
    send_halo(ext0, ITERS, rows_sides)
    for i in (1, 2, 3, 5):
        copies[i].wait()

    for a in range(rows_y):
        lanes = lax.broadcasted_iota(jnp.int32, (cols_z, cols_z), 1)
        subs = lax.broadcasted_iota(jnp.int32, (cols_z, cols_z), 0)
        counts = jnp.sum(
            jnp.where(lanes == subs, cnt_ref[0, pl.ds(a, 1), :], 0).astype(jnp.float32),
            axis=1,
            keepdims=True,
        )
        places = lax.broadcasted_iota(jnp.int32, (cols_z, SLOTS), 1).astype(jnp.float32)
        for c in range(SLOTS):
            hit = (list_ref[0, a] == c) & (places < counts)
            active = jnp.sum(jnp.where(hit, 1.0, 0.0), axis=1, keepdims=True)
            mask[c, a] = jnp.broadcast_to((1.0 - active) * OFF, (cols_z, PB))

    def own_columns(a, b):
        cols = jnp.transpose(own8[a, b])
        cx = jnp.broadcast_to(cols[:, 0:1], (PB, PB))
        cy = jnp.broadcast_to(cols[:, 1:2], (PB, PB))
        cz = jnp.broadcast_to(cols[:, 2:3], (PB, PB))
        return cx, cy, cz, -(cx * cx + cy * cy + cz * cz)

    def make_weights(a, b, pairs):
        cx, cy, cz, cn = own_columns(a, b)
        for dy, dz in pairs:
            c = 3 * (dy + 1) + (dz + 1)
            near = ext0[1 + a + dy, 1 + b + dz]
            rx = near[0:1]
            ry = near[1:2] + 2.0 * KAPPA * dy
            rz = near[2:3] + 2.0 * KAPPA * dz
            rn = mask[c, a, pl.ds(b, 1), :] - 0.25 * (rx * rx + ry * ry + rz * rz)
            wts[a, b, c] = jnp.exp2((cn + rn) + (cx * rx + cy * ry) + cz * rz)

    all_dz = (-1, 0, 1)

    def inner(b, carry):
        for a in range(rows_y):
            dys = [dy for dy in (-1, 0, 1) if 0 <= a + dy < rows_y]
            make_weights(a, b, [(dy, dz) for dy in dys for dz in all_dz])
        return carry

    def outer(b, carry):
        for a in range(rows_y):
            dys = [dy for dy in (-1, 0, 1) if not 0 <= a + dy < rows_y]
            make_weights(a, b, [(dy, dz) for dy in dys for dz in all_dz])
        return carry

    def ends(far):
        for b, out in ((0, -1), (cols_z - 1, 1)):
            for a in range(rows_y):
                dzs = [dz for dz in all_dz if (dz == out) == far]
                make_weights(a, b, [(dy, dz) for dy in (-1, 0, 1) for dz in dzs])

    def deliver(values, sweep):
        hi = values.astype(jnp.bfloat16)
        low = (values - hi.astype(jnp.float32)).astype(jnp.bfloat16)
        both = jnp.concatenate([hi, low], axis=0)
        total = jnp.dot(onehot[...], both, preferred_element_type=jnp.float32)
        buckets[sweep] = total.reshape(n_near, guards, PB)
        send_buckets(sweep)

    def sums(near_row, with_den, low, high):
        def body(b, carry):
            rows = [[near_row(e, b + k) for k in range(3)] for e in range(rows_y + 2)]
            for a in range(rows_y):
                acc = None
                tot = None
                for c in range(SLOTS):
                    w = wts[a, b, c]
                    part = w * rows[a + c // 3][c % 3]
                    acc = part if acc is None else acc + part
                    if with_den:
                        tot = w if tot is None else tot + w
                num[a, pl.ds(b, 1), :] = row_sums(acc)
                if with_den:
                    den[a, pl.ds(b, 1), :] = row_sums(tot)
            return carry

        lax.fori_loop(low, high, body, 0)

    lax.fori_loop(1, cols_z - 1, inner, 0)
    pl.semaphore_wait(known, len(tellers))
    send_halo(ext0, 0, far_sides)
    rim_wait(ext0, h_recv.at[ITERS], rows_rim)
    middle = cols_z // 2
    lax.fori_loop(1, middle, outer, 0)
    whole_wait(got_first, g_recv.at[0])
    entries = 2 * n_gy * slots_out
    dest = n_near * guards
    code_rows = got_first[:, pl.ds(slots_out, slots_out), :].reshape(entries, PB)[:, :dest]
    lane = lax.broadcasted_iota(jnp.int32, (entries, dest), 1)
    wanted = (y * n_gz + half * n_near) * guards + lane
    hits = jnp.where(code_rows == wanted.astype(jnp.float32), 1.0, 0.0)
    chosen = jnp.transpose(hits).astype(jnp.bfloat16)
    onehot[...] = jnp.concatenate([chosen, chosen], axis=1)
    deliver(got_first[:, pl.ds(0, slots_out), :].reshape(entries, PB), 0)

    lax.fori_loop(middle, cols_z - 1, outer, 0)
    ends(False)

    def start_row(e, k):
        return ext0[e, k, pl.ds(3, 1), :]

    sums(start_row, True, 1, cols_z - 1)
    rim_wait(ext0, h_recv.at[0], far_rim)
    ends(True)
    sums(start_row, True, 0, 1)
    sums(start_row, True, cols_z - 1, cols_z)
    coef = gc_ref[0, 0, 0].reshape(rows_y, cols_z, PB)
    scale = 1.0 / (den[...] + coef + 1.0)

    for sweep in range(ITERS):
        base = num[...] - src_ref[0]
        whole_wait(got_buckets.at[sweep], r_recv.at[sweep])
        mine = buckets[sweep, near]
        for o in range(n_near - 1):
            mine = mine + got_buckets[sweep, o]
        new = (base + coef * mine.reshape(rows_y, cols_z, PB)) * scale
        if sweep == ITERS - 1:
            out_ref[0] = new
            break
        pden[...] = new.reshape(rows_y * cols_z, PB)
        interpolate(later.at[sweep])
        send_values(later.at[sweep], got.at[sweep], sweep + 1)
        press = pext.at[sweep]
        for a in range(rows_y):
            for b in range(cols_z):
                press[1 + a, 1 + b] = new[a, b : b + 1]
        send_halo(press, sweep + 1, sides)
        whole_wait(got.at[sweep], g_recv.at[sweep + 1])
        deliver(got[sweep].reshape(entries, PB), sweep + 1)
        rim_wait(press, h_recv.at[sweep + 1], rows_rim + far_rim)
        sums(lambda e, k: press[e, k], False, 0, cols_z)

    rim_wait(ext0, h_send.at[ITERS], rows_rim)
    rim_wait(ext0, h_send.at[0], far_rim)
    whole_wait(got_first, g_send.at[0])
    for sweep in range(ITERS):
        whole_wait(got_buckets.at[sweep], r_send.at[sweep])
        if sweep:
            rim_wait(pext.at[sweep - 1], h_send.at[sweep], rows_rim + far_rim)
            whole_wait(got.at[sweep - 1], g_send.at[sweep])


def local(n_gy, n_gz, *args):
    args = (jnp.swapaxes(args[0], 2, 3),) + args[1:]
    guard_coef, send_block = args[5], args[6]
    rows_y, cols_z = args[3].shape[1:3]
    guards = guard_coef.shape[3]
    slots_out = send_block.shape[3]
    n_near = n_gz // 2
    f32 = jnp.float32
    dma = pltpu.SemaphoreType.DMA((ITERS,))
    halo_dma = pltpu.SemaphoreType.DMA((ITERS + 1,))
    spaces = [pltpu.VMEM] * 6 + [pltpu.SMEM] * 4 + [pltpu.VMEM]
    return pl.pallas_call(
        functools.partial(kernel, n_gy, n_gz),
        out_shape=pltpu.VMEM((1, rows_y, cols_z, PB), f32),
        in_specs=[pl.BlockSpec(memory_space=pl.ANY)] * len(args),
        out_specs=pl.BlockSpec(memory_space=pltpu.VMEM),
        scratch_shapes=[space(a.shape, a.dtype) for space, a in zip(spaces, args)]
        + [
            pltpu.VMEM((rows_y + 2, cols_z + 2, 4, PB), f32),
            pltpu.VMEM((rows_y, cols_z, 8, PB), f32),
            pltpu.VMEM((ITERS - 1, rows_y + 2, cols_z + 2, 1, PB), f32),
            pltpu.VMEM((rows_y * cols_z, PB), f32),
            pltpu.VMEM((rows_y, cols_z, SLOTS, PB, PB), f32),
            pltpu.VMEM((SLOTS, rows_y, cols_z, PB), f32),
            pltpu.VMEM((2 * slots_out, PB), f32),
            pltpu.VMEM((ITERS - 1, slots_out, PB), f32),
            pltpu.VMEM((2 * n_gy, 2 * slots_out, PB), f32),
            pltpu.VMEM((ITERS - 1, 2 * n_gy, slots_out, PB), f32),
            pltpu.VMEM((ITERS, n_near, guards, PB), f32),
            pltpu.VMEM((ITERS, n_near - 1, guards, PB), f32),
            pltpu.VMEM((n_near * guards, 4 * n_gy * slots_out), jnp.bfloat16),
            pltpu.VMEM((rows_y, cols_z, PB), f32),
            pltpu.VMEM((rows_y, cols_z, PB), f32),
            halo_dma,
            halo_dma,
            dma,
            dma,
            dma,
            dma,
            pltpu.SemaphoreType.DMA((len(args),)),
            pltpu.SemaphoreType.REGULAR,
        ],
        compiler_params=pltpu.CompilerParams(
            collective_id=0, has_side_effects=True, vmem_limit_bytes=60 * 1024 * 1024
        ),
    )(*args)


def solution(mesh):
    placed = (
        P("grp", "gy", "gz", None, None),
        P("grp", "gy", "gz", None),
        P("grp", "gy", "gz"),
        P("grp", "gy", "gz", None),
        P("grp", "gy", "gz", None),
        P("grp", "gy", "gz", None, None),
        P("grp", "gy", "gz", None),
        P("grp", "gy", "gz", None),
        P("grp", "gy", "gz", None),
        P("grp", "gy", "gz"),
        P("grp", "gy", "gz", None, None, None),
    )
    return jax.shard_map(
        functools.partial(local, mesh.shape["gy"], mesh.shape["gz"]),
        mesh=mesh,
        in_specs=placed,
        out_specs=P("grp", "gy", "gz", None),
        check_vma=False,
    )
```

```python
import functools
import math

import jax
import jax.numpy as jnp
from jax import lax
from jax.experimental import pallas as pl
from jax.experimental.pallas import tpu as pltpu
from jax.sharding import PartitionSpec as P

PB = 128
SLOTS = 9
ITERS = 3
KERNEL_WIDTH = 0.5
MESH = pl.DeviceIdType.MESH
KAPPA = math.sqrt(1.0 / (KERNEL_WIDTH * math.log(2.0)))
OFF = -1.0e4


def kernel(
    n_gy,
    n_gz,
    *refs,
):
    sources, out_ref, held, rest = refs[:11], refs[11], refs[12:23], refs[23:]
    off_ref, list_ref, cnt_ref, src_ref, p_ref, gc_ref = held[:6]
    sb_ref, st_ref, sg_ref, sc_ref, interp_ref = held[6:]
    (
        ext0,
        own8,
        pext,
        pden,
        wts,
        mask,
        first,
        later,
        got_first,
        got,
        buckets,
        got_buckets,
        onehot,
        num,
        den,
        h_send,
        h_recv,
        g_send,
        g_recv,
        r_send,
        r_recv,
        in_sem,
        known,
    ) = rest
    g = lax.axis_index("grp")
    y = lax.axis_index("gy")
    z = lax.axis_index("gz")
    rows_y, cols_z = off_ref.shape[1], off_ref.shape[3]
    n_near = n_gz // 2
    half, near = z // n_near, lax.rem(z, n_near)
    guards = gc_ref.shape[3]
    slots_out = sb_ref.shape[3]

    def at(gg, dy, dz):
        return (gg, lax.rem(y + dy + n_gy, n_gy), lax.rem(z + dz + n_gz, n_gz))

    across = [o for o in (4, 5, 6, 7, 2, 3, 1, 0) if o < n_gy]
    stage1 = [(o, 1) for o in across[:6]] + [(o, 0) for o in across[:4]]
    stage1 += [(o, 1) for o in across[6:]] + [(o, 0) for o in across[4:]]
    stage2 = [o for o in (4, 5, 7, 6, 3, 2, 1) if o < n_near]

    def at1(o, f):
        return (1 - g, y ^ o, (half ^ f) * n_near + near)

    def at2(o):
        return (g, y, half * n_near + (near ^ o))

    copies = [
        pltpu.make_async_copy(src, dst, in_sem.at[i])
        for i, (src, dst) in enumerate(zip(sources, held))
    ]
    for i in (4, 6, 10):
        copies[i].start()
    barrier = pltpu.get_barrier_semaphore()
    farthest = n_near // 2
    beside = [at(g, 1, 0), at(g, -1, 0)]
    beside += [
        (g, lax.rem(y + a + n_gy, n_gy), (half ^ 1) * n_near + near) for a in (-1, 0, 1)
    ]
    people = [at1(*of) for of in stage1] + [at2(o) for o in stage2 if o != farthest] + beside
    tellers = beside + [at2(1)]
    for who in people:
        pl.semaphore_signal(barrier, inc=1, device_id=who, device_id_type=MESH)
    for i in (7, 8, 9, 0, 1, 2, 3, 5):
        copies[i].start()

    sides = []
    for dy in (-1, 0, 1):
        for dz in (-1, 0, 1):
            if (dy, dz) == (0, 0):
                continue
            ys = {-1: (1, 1), 0: (1, rows_y), 1: (rows_y, 1)}[dy]
            zs = {-1: (1, 1), 0: (1, cols_z), 1: (cols_z, 1)}[dz]
            yd = {-1: rows_y + 1, 0: 1, 1: 0}[dy]
            zd = {-1: cols_z + 1, 0: 1, 1: 0}[dz]
            sides.append((dy, dz, ys, zs, yd, zd))

    def send_halo(buf, sem, which):
        for dy, dz, ys, zs, yd, zd in which:
            pltpu.make_async_remote_copy(
                src_ref=buf.at[pl.ds(ys[0], ys[1]), pl.ds(zs[0], zs[1])],
                dst_ref=buf.at[pl.ds(yd, ys[1]), pl.ds(zd, zs[1])],
                send_sem=h_send.at[sem],
                recv_sem=h_recv.at[sem],
                device_id=at(g, dy, dz),
                device_id_type=MESH,
            ).start()

    rows_sides = [s for s in sides if s[1] == 0]
    far_sides = [s for s in sides if s[1] != 0]

    def rim_wait(buf, sem, blocks):
        part = buf.at[pl.ds(0, blocks // cols_z), pl.ds(0, cols_z)]
        pltpu.make_async_copy(part, part, sem).wait()

    rows_rim = 2 * cols_z
    far_rim = 2 * rows_y + 4

    def send_values(src, dst, sweep):
        for o, f in stage1:
            pltpu.make_async_remote_copy(
                src_ref=src,
                dst_ref=dst.at[2 * o + f],
                send_sem=g_send.at[sweep],
                recv_sem=g_recv.at[sweep],
                device_id=at1(o, f),
                device_id_type=MESH,
            ).start()

    def send_buckets(sweep):
        for o in stage2:
            pltpu.make_async_remote_copy(
                src_ref=buckets.at[sweep, near ^ o],
                dst_ref=got_buckets.at[sweep, o - 1],
                send_sem=r_send.at[sweep],
                recv_sem=r_recv.at[sweep],
                device_id=at2(o),
                device_id_type=MESH,
            ).start()

    def whole_wait(ref, sem):
        pltpu.make_async_copy(ref, ref, sem).wait()

    row_id = lax.broadcasted_iota(jnp.int32, (PB, PB), 0)
    lane_id = lax.broadcasted_iota(jnp.int32, (PB, PB), 1)
    eye = row_id == lane_id

    def row_sums(acc):
        total = jnp.sum(acc, axis=1, keepdims=True)
        return jnp.sum(jnp.where(eye, total, 0.0), axis=0, keepdims=True)

    def interpolate(dst):
        for s in range(slots_out):
            press = pden[pl.ds(sb_ref[0, 0, 0, s], 1), :]
            dst[pl.ds(s, 1), :] = row_sums(interp_ref[0, 0, 0, s] * press)

    for i in (4, 6):
        copies[i].wait()
    for a in range(rows_y):
        pden[pl.ds(a * cols_z, cols_z), :] = p_ref[0, a]
    copies[10].wait()
    interpolate(first)
    for i in (7, 8, 9):
        copies[i].wait()
    codes = jnp.full((slots_out, PB), -1, jnp.int32)
    slot_row = lax.broadcasted_iota(jnp.int32, (slots_out, PB), 0)
    for s in range(slots_out):
        codes = jnp.where(slot_row == s, st_ref[0, 0, 0, s] * guards + sg_ref[0, 0, 0, s], codes)
    codes = jnp.where(slot_row < sc_ref[0, 0, 0], codes, -1)
    first[pl.ds(slots_out, slots_out), :] = codes.astype(jnp.float32)

    pl.semaphore_wait(barrier, len(people))
    for who in tellers:
        pl.semaphore_signal(known, inc=1, device_id=who, device_id_type=MESH)
    send_values(first, got_first, 0)

    copies[0].wait()
    for a in range(rows_y):
        for k in range(3):
            scaled = (off_ref[0, a, k] - 0.5) * (2.0 * KAPPA)
            for b in range(cols_z):
                ext0[1 + a, 1 + b, pl.ds(k, 1), :] = scaled[b : b + 1]
                own8[a, b, pl.ds(k, 1), :] = 0.5 * scaled[b : b + 1]
        for b in range(cols_z):
            ext0[1 + a, 1 + b, pl.ds(3, 1), :] = p_ref[0, a, pl.ds(b, 1), :]
    send_halo(ext0, ITERS, rows_sides)
    for i in (1, 2, 3, 5):
        copies[i].wait()

    for a in range(rows_y):
        lanes = lax.broadcasted_iota(jnp.int32, (cols_z, cols_z), 1)
        subs = lax.broadcasted_iota(jnp.int32, (cols_z, cols_z), 0)
        counts = jnp.sum(
            jnp.where(lanes == subs, cnt_ref[0, pl.ds(a, 1), :], 0).astype(jnp.float32),
            axis=1,
            keepdims=True,
        )
        places = lax.broadcasted_iota(jnp.int32, (cols_z, SLOTS), 1).astype(jnp.float32)
        for c in range(SLOTS):
            hit = (list_ref[0, a] == c) & (places < counts)
            active = jnp.sum(jnp.where(hit, 1.0, 0.0), axis=1, keepdims=True)
            mask[c, a] = jnp.broadcast_to((1.0 - active) * OFF, (cols_z, PB))

    def own_columns(a, b):
        cols = jnp.transpose(own8[a, b])
        cx = jnp.broadcast_to(cols[:, 0:1], (PB, PB))
        cy = jnp.broadcast_to(cols[:, 1:2], (PB, PB))
        cz = jnp.broadcast_to(cols[:, 2:3], (PB, PB))
        return cx, cy, cz, -(cx * cx + cy * cy + cz * cz)

    def make_weights(a, b, pairs):
        cx, cy, cz, cn = own_columns(a, b)
        for dy, dz in pairs:
            c = 3 * (dy + 1) + (dz + 1)
            near = ext0[1 + a + dy, 1 + b + dz]
            rx = near[0:1]
            ry = near[1:2] + 2.0 * KAPPA * dy
            rz = near[2:3] + 2.0 * KAPPA * dz
            rn = mask[c, a, pl.ds(b, 1), :] - 0.25 * (rx * rx + ry * ry + rz * rz)
            wts[a, b, c] = jnp.exp2((cn + rn) + (cx * rx + cy * ry) + cz * rz)

    all_dz = (-1, 0, 1)

    def inner(b, carry):
        for a in range(rows_y):
            dys = [dy for dy in (-1, 0, 1) if 0 <= a + dy < rows_y]
            make_weights(a, b, [(dy, dz) for dy in dys for dz in all_dz])
        return carry

    def outer(b, carry):
        for a in range(rows_y):
            dys = [dy for dy in (-1, 0, 1) if not 0 <= a + dy < rows_y]
            make_weights(a, b, [(dy, dz) for dy in dys for dz in all_dz])
        return carry

    def ends(far):
        for b, out in ((0, -1), (cols_z - 1, 1)):
            for a in range(rows_y):
                dzs = [dz for dz in all_dz if (dz == out) == far]
                make_weights(a, b, [(dy, dz) for dy in (-1, 0, 1) for dz in dzs])

    def deliver(values, sweep):
        hi = values.astype(jnp.bfloat16)
        low = (values - hi.astype(jnp.float32)).astype(jnp.bfloat16)
        both = jnp.concatenate([hi, low], axis=0)
        total = jnp.dot(onehot[...], both, preferred_element_type=jnp.float32)
        buckets[sweep] = total.reshape(n_near, guards, PB)
        send_buckets(sweep)

    def sums(near_row, with_den, low, high):
        def body(b, carry):
            rows = [[near_row(e, b + k) for k in range(3)] for e in range(rows_y + 2)]
            for a in range(rows_y):
                acc = None
                tot = None
                for c in range(SLOTS):
                    w = wts[a, b, c]
                    part = w * rows[a + c // 3][c % 3]
                    acc = part if acc is None else acc + part
                    if with_den:
                        tot = w if tot is None else tot + w
                num[a, pl.ds(b, 1), :] = row_sums(acc)
                if with_den:
                    den[a, pl.ds(b, 1), :] = row_sums(tot)
            return carry

        lax.fori_loop(low, high, body, 0)

    lax.fori_loop(1, cols_z - 1, inner, 0)
    pl.semaphore_wait(known, len(tellers))
    send_halo(ext0, 0, far_sides)
    rim_wait(ext0, h_recv.at[ITERS], rows_rim)
    middle = cols_z // 2
    lax.fori_loop(1, middle, outer, 0)
    whole_wait(got_first, g_recv.at[0])
    entries = 2 * n_gy * slots_out
    dest = n_near * guards
    code_rows = got_first[:, pl.ds(slots_out, slots_out), :].reshape(entries, PB)[:, :dest]
    lane = lax.broadcasted_iota(jnp.int32, (entries, dest), 1)
    wanted = (y * n_gz + half * n_near) * guards + lane
    hits = jnp.where(code_rows == wanted.astype(jnp.float32), 1.0, 0.0)
    chosen = jnp.transpose(hits).astype(jnp.bfloat16)
    onehot[...] = jnp.concatenate([chosen, chosen], axis=1)
    deliver(got_first[:, pl.ds(0, slots_out), :].reshape(entries, PB), 0)

    lax.fori_loop(middle, cols_z - 1, outer, 0)
    ends(False)

    def start_row(e, k):
        return ext0[e, k, pl.ds(3, 1), :]

    sums(start_row, True, 1, cols_z - 1)
    rim_wait(ext0, h_recv.at[0], far_rim)
    ends(True)
    sums(start_row, True, 0, 1)
    sums(start_row, True, cols_z - 1, cols_z)
    coef = gc_ref[0, 0, 0].reshape(rows_y, cols_z, PB)
    scale = 1.0 / (den[...] + coef + 1.0)

    def updated(sweep):
        base = num[...] - src_ref[0]
        whole_wait(got_buckets.at[sweep], r_recv.at[sweep])
        mine = buckets[sweep, near]
        for o in range(n_near - 1):
            mine = mine + got_buckets[sweep, o]
        return (base + coef * mine.reshape(rows_y, cols_z, PB)) * scale

    def one_sweep(sweep, carry):
        new = updated(sweep)
        pden[...] = new.reshape(rows_y * cols_z, PB)
        interpolate(later.at[sweep])
        send_values(later.at[sweep], got.at[sweep], sweep + 1)
        press = pext.at[sweep]
        for a in range(rows_y):
            for b in range(cols_z):
                press[1 + a, 1 + b] = new[a, b : b + 1]
        send_halo(press, sweep + 1, sides)
        whole_wait(got.at[sweep], g_recv.at[sweep + 1])
        deliver(got[sweep].reshape(entries, PB), sweep + 1)
        rim_wait(press, h_recv.at[sweep + 1], rows_rim + far_rim)
        sums(lambda e, k: press[e, k], False, 0, cols_z)
        return carry

    lax.fori_loop(0, ITERS - 1, one_sweep, 0)
    out_ref[0] = updated(ITERS - 1)

    rim_wait(ext0, h_send.at[ITERS], rows_rim)
    rim_wait(ext0, h_send.at[0], far_rim)
    whole_wait(got_first, g_send.at[0])
    for sweep in range(ITERS):
        whole_wait(got_buckets.at[sweep], r_send.at[sweep])
        if sweep:
            rim_wait(pext.at[sweep - 1], h_send.at[sweep], rows_rim + far_rim)
            whole_wait(got.at[sweep - 1], g_send.at[sweep])


def local(n_gy, n_gz, *args):
    args = (jnp.swapaxes(args[0], 2, 3),) + args[1:]
    guard_coef, send_block = args[5], args[6]
    rows_y, cols_z = args[3].shape[1:3]
    guards = guard_coef.shape[3]
    slots_out = send_block.shape[3]
    n_near = n_gz // 2
    f32 = jnp.float32
    dma = pltpu.SemaphoreType.DMA((ITERS,))
    halo_dma = pltpu.SemaphoreType.DMA((ITERS + 1,))
    spaces = [pltpu.VMEM] * 6 + [pltpu.SMEM] * 4 + [pltpu.VMEM]
    return pl.pallas_call(
        functools.partial(kernel, n_gy, n_gz),
        out_shape=pltpu.VMEM((1, rows_y, cols_z, PB), f32),
        in_specs=[pl.BlockSpec(memory_space=pl.ANY)] * len(args),
        out_specs=pl.BlockSpec(memory_space=pltpu.VMEM),
        scratch_shapes=[space(a.shape, a.dtype) for space, a in zip(spaces, args)]
        + [
            pltpu.VMEM((rows_y + 2, cols_z + 2, 4, PB), f32),
            pltpu.VMEM((rows_y, cols_z, 8, PB), f32),
            pltpu.VMEM((ITERS - 1, rows_y + 2, cols_z + 2, 1, PB), f32),
            pltpu.VMEM((rows_y * cols_z, PB), f32),
            pltpu.VMEM((rows_y, cols_z, SLOTS, PB, PB), f32),
            pltpu.VMEM((SLOTS, rows_y, cols_z, PB), f32),
            pltpu.VMEM((2 * slots_out, PB), f32),
            pltpu.VMEM((ITERS - 1, slots_out, PB), f32),
            pltpu.VMEM((2 * n_gy, 2 * slots_out, PB), f32),
            pltpu.VMEM((ITERS - 1, 2 * n_gy, slots_out, PB), f32),
            pltpu.VMEM((ITERS, n_near, guards, PB), f32),
            pltpu.VMEM((ITERS, n_near - 1, guards, PB), f32),
            pltpu.VMEM((n_near * guards, 4 * n_gy * slots_out), jnp.bfloat16),
            pltpu.VMEM((rows_y, cols_z, PB), f32),
            pltpu.VMEM((rows_y, cols_z, PB), f32),
            halo_dma,
            halo_dma,
            dma,
            dma,
            dma,
            dma,
            pltpu.SemaphoreType.DMA((len(args),)),
            pltpu.SemaphoreType.REGULAR,
        ],
        compiler_params=pltpu.CompilerParams(
            collective_id=0, has_side_effects=True, vmem_limit_bytes=60 * 1024 * 1024
        ),
    )(*args)


def solution(mesh):
    placed = (
        P("grp", "gy", "gz", None, None),
        P("grp", "gy", "gz", None),
        P("grp", "gy", "gz"),
        P("grp", "gy", "gz", None),
        P("grp", "gy", "gz", None),
        P("grp", "gy", "gz", None, None),
        P("grp", "gy", "gz", None),
        P("grp", "gy", "gz", None),
        P("grp", "gy", "gz", None),
        P("grp", "gy", "gz"),
        P("grp", "gy", "gz", None, None, None),
    )
    return jax.shard_map(
        functools.partial(local, mesh.shape["gy"], mesh.shape["gz"]),
        mesh=mesh,
        in_specs=placed,
        out_specs=P("grp", "gy", "gz", None),
        check_vma=False,
    )
```

```python
import functools
import math

import jax
import jax.numpy as jnp
from jax import lax
from jax.experimental import pallas as pl
from jax.experimental.pallas import tpu as pltpu
from jax.sharding import PartitionSpec as P

PB = 128
SLOTS = 9
ITERS = 3
KERNEL_WIDTH = 0.5
MESH = pl.DeviceIdType.MESH
KAPPA = math.sqrt(1.0 / (KERNEL_WIDTH * math.log(2.0)))
OFF = -1.0e4


def kernel(
    n_gy,
    n_gz,
    *refs,
):
    sources, out_ref, held, rest = refs[:11], refs[11], refs[12:23], refs[23:]
    off_ref, list_ref, cnt_ref, src_ref, p_ref, gc_ref = held[:6]
    sb_ref, st_ref, sg_ref, sc_ref, interp_ref = held[6:]
    (
        ext0,
        own8,
        pext,
        pden,
        wts,
        mask,
        first,
        later,
        got_first,
        got,
        buckets,
        got_buckets,
        onehot,
        num,
        den,
        h_send,
        h_recv,
        g_send,
        g_recv,
        r_send,
        r_recv,
        in_sem,
        known,
        far_bucket,
    ) = rest
    g = lax.axis_index("grp")
    y = lax.axis_index("gy")
    z = lax.axis_index("gz")
    rows_y, cols_z = off_ref.shape[1], off_ref.shape[3]
    n_near = n_gz // 2
    half, near = z // n_near, lax.rem(z, n_near)
    guards = gc_ref.shape[3]
    slots_out = sb_ref.shape[3]

    def at(gg, dy, dz):
        return (gg, lax.rem(y + dy + n_gy, n_gy), lax.rem(z + dz + n_gz, n_gz))

    across = [o for o in (4, 5, 6, 7, 2, 3, 1, 0) if o < n_gy]
    stage1 = [(o, 1) for o in across[:6]] + [(o, 0) for o in across[:4]]
    stage1 += [(o, 1) for o in across[6:]] + [(o, 0) for o in across[4:]]
    stage2 = [o for o in (4, 5, 7, 6, 3, 2, 1) if o < n_near]

    def at1(o, f):
        return (1 - g, y ^ o, (half ^ f) * n_near + near)

    def at2(o):
        return (g, y, half * n_near + (near ^ o))

    copies = [
        pltpu.make_async_copy(src, dst, in_sem.at[i])
        for i, (src, dst) in enumerate(zip(sources, held))
    ]
    for i in (4, 6, 10):
        copies[i].start()
    barrier = pltpu.get_barrier_semaphore()
    farthest = n_near // 2
    beside = [at(g, 1, 0), at(g, -1, 0)]
    beside += [
        (g, lax.rem(y + a + n_gy, n_gy), (half ^ 1) * n_near + near) for a in (-1, 0, 1)
    ]
    people = [at1(*of) for of in stage1] + [at2(o) for o in stage2 if o != farthest] + beside
    tellers = beside + [at2(1)]
    for who in people:
        pl.semaphore_signal(barrier, inc=1, device_id=who, device_id_type=MESH)
    for i in (7, 8, 9, 0, 1, 2, 3, 5):
        copies[i].start()

    sides = []
    for dy in (-1, 0, 1):
        for dz in (-1, 0, 1):
            if (dy, dz) == (0, 0):
                continue
            ys = {-1: (1, 1), 0: (1, rows_y), 1: (rows_y, 1)}[dy]
            zs = {-1: (1, 1), 0: (1, cols_z), 1: (cols_z, 1)}[dz]
            yd = {-1: rows_y + 1, 0: 1, 1: 0}[dy]
            zd = {-1: cols_z + 1, 0: 1, 1: 0}[dz]
            sides.append((dy, dz, ys, zs, yd, zd))

    def send_halo(buf, sem, which):
        for dy, dz, ys, zs, yd, zd in which:
            pltpu.make_async_remote_copy(
                src_ref=buf.at[pl.ds(ys[0], ys[1]), pl.ds(zs[0], zs[1])],
                dst_ref=buf.at[pl.ds(yd, ys[1]), pl.ds(zd, zs[1])],
                send_sem=h_send.at[sem],
                recv_sem=h_recv.at[sem],
                device_id=at(g, dy, dz),
                device_id_type=MESH,
            ).start()

    rows_sides = [s for s in sides if s[1] == 0]
    far_sides = [s for s in sides if s[1] != 0]

    def rim_wait(buf, sem, blocks):
        part = buf.at[pl.ds(0, blocks // cols_z), pl.ds(0, cols_z)]
        pltpu.make_async_copy(part, part, sem).wait()

    rows_rim = 2 * cols_z
    far_rim = 2 * rows_y + 4

    def send_values(src, dst, sweep):
        for o, f in stage1:
            pltpu.make_async_remote_copy(
                src_ref=src,
                dst_ref=dst.at[2 * o + f],
                send_sem=g_send.at[sweep],
                recv_sem=g_recv.at[sweep],
                device_id=at1(o, f),
                device_id_type=MESH,
            ).start()

    def send_bucket(src, o, sweep):
        pltpu.make_async_remote_copy(
            src_ref=src,
            dst_ref=got_buckets.at[sweep, o - 1],
            send_sem=r_send.at[sweep],
            recv_sem=r_recv.at[sweep],
            device_id=at2(o),
            device_id_type=MESH,
        ).start()

    def whole_wait(ref, sem):
        pltpu.make_async_copy(ref, ref, sem).wait()

    row_id = lax.broadcasted_iota(jnp.int32, (PB, PB), 0)
    lane_id = lax.broadcasted_iota(jnp.int32, (PB, PB), 1)
    eye = row_id == lane_id

    def row_sums(acc):
        total = jnp.sum(acc, axis=1, keepdims=True)
        return jnp.sum(jnp.where(eye, total, 0.0), axis=0, keepdims=True)

    def interpolate(dst):
        for s in range(slots_out):
            press = pden[pl.ds(sb_ref[0, 0, 0, s], 1), :]
            dst[pl.ds(s, 1), :] = row_sums(interp_ref[0, 0, 0, s] * press)

    for i in (4, 6):
        copies[i].wait()
    for a in range(rows_y):
        pden[pl.ds(a * cols_z, cols_z), :] = p_ref[0, a]
    copies[10].wait()
    interpolate(first)
    for i in (7, 8, 9):
        copies[i].wait()
    codes = jnp.full((slots_out, PB), -1, jnp.int32)
    slot_row = lax.broadcasted_iota(jnp.int32, (slots_out, PB), 0)
    for s in range(slots_out):
        codes = jnp.where(slot_row == s, st_ref[0, 0, 0, s] * guards + sg_ref[0, 0, 0, s], codes)
    codes = jnp.where(slot_row < sc_ref[0, 0, 0], codes, -1)
    first[pl.ds(slots_out, slots_out), :] = codes.astype(jnp.float32)

    pl.semaphore_wait(barrier, len(people))
    for who in tellers:
        pl.semaphore_signal(known, inc=1, device_id=who, device_id_type=MESH)
    send_values(first, got_first, 0)

    copies[0].wait()
    for a in range(rows_y):
        for k in range(3):
            scaled = (off_ref[0, a, k] - 0.5) * (2.0 * KAPPA)
            for b in range(cols_z):
                ext0[1 + a, 1 + b, pl.ds(k, 1), :] = scaled[b : b + 1]
                own8[a, b, pl.ds(k, 1), :] = 0.5 * scaled[b : b + 1]
        for b in range(cols_z):
            ext0[1 + a, 1 + b, pl.ds(3, 1), :] = p_ref[0, a, pl.ds(b, 1), :]
    send_halo(ext0, ITERS, rows_sides)
    for i in (1, 2, 3, 5):
        copies[i].wait()

    for a in range(rows_y):
        lanes = lax.broadcasted_iota(jnp.int32, (cols_z, cols_z), 1)
        subs = lax.broadcasted_iota(jnp.int32, (cols_z, cols_z), 0)
        counts = jnp.sum(
            jnp.where(lanes == subs, cnt_ref[0, pl.ds(a, 1), :], 0).astype(jnp.float32),
            axis=1,
            keepdims=True,
        )
        places = lax.broadcasted_iota(jnp.int32, (cols_z, SLOTS), 1).astype(jnp.float32)
        for c in range(SLOTS):
            hit = (list_ref[0, a] == c) & (places < counts)
            active = jnp.sum(jnp.where(hit, 1.0, 0.0), axis=1, keepdims=True)
            mask[c, a] = jnp.broadcast_to((1.0 - active) * OFF, (cols_z, PB))

    def own_columns(a, b):
        cols = jnp.transpose(own8[a, b])
        cx = jnp.broadcast_to(cols[:, 0:1], (PB, PB))
        cy = jnp.broadcast_to(cols[:, 1:2], (PB, PB))
        cz = jnp.broadcast_to(cols[:, 2:3], (PB, PB))
        return cx, cy, cz, -(cx * cx + cy * cy + cz * cz)

    def make_weights(a, b, pairs):
        cx, cy, cz, cn = own_columns(a, b)
        for dy, dz in pairs:
            c = 3 * (dy + 1) + (dz + 1)
            near = ext0[1 + a + dy, 1 + b + dz]
            rx = near[0:1]
            ry = near[1:2] + 2.0 * KAPPA * dy
            rz = near[2:3] + 2.0 * KAPPA * dz
            rn = mask[c, a, pl.ds(b, 1), :] - 0.25 * (rx * rx + ry * ry + rz * rz)
            wts[a, b, c] = jnp.exp2((cn + rn) + (cx * rx + cy * ry) + cz * rz)

    all_dz = (-1, 0, 1)

    def inner(b, carry):
        for a in range(rows_y):
            dys = [dy for dy in (-1, 0, 1) if 0 <= a + dy < rows_y]
            make_weights(a, b, [(dy, dz) for dy in dys for dz in all_dz])
        return carry

    def outer(b, carry):
        for a in range(rows_y):
            dys = [dy for dy in (-1, 0, 1) if not 0 <= a + dy < rows_y]
            make_weights(a, b, [(dy, dz) for dy in dys for dz in all_dz])
        return carry

    def ends(far):
        for b, out in ((0, -1), (cols_z - 1, 1)):
            for a in range(rows_y):
                dzs = [dz for dz in all_dz if (dz == out) == far]
                make_weights(a, b, [(dy, dz) for dy in (-1, 0, 1) for dz in dzs])

    def deliver(values, sweep):
        hi = values.astype(jnp.bfloat16)
        low = (values - hi.astype(jnp.float32)).astype(jnp.bfloat16)
        both = jnp.concatenate([hi, low], axis=0)
        o = stage2[0]
        rows = pl.ds(pl.multiple_of((near ^ o) * guards, guards), guards)
        far_bucket[sweep] = jnp.dot(onehot[rows, :], both, preferred_element_type=jnp.float32)
        send_bucket(far_bucket.at[sweep], o, sweep)
        total = jnp.dot(onehot[...], both, preferred_element_type=jnp.float32)
        buckets[sweep] = total.reshape(n_near, guards, PB)
        for o in stage2[1:]:
            send_bucket(buckets.at[sweep, near ^ o], o, sweep)

    def sums(near_row, with_den, low, high):
        def body(b, carry):
            rows = [[near_row(e, b + k) for k in range(3)] for e in range(rows_y + 2)]
            for a in range(rows_y):
                acc = None
                tot = None
                for c in range(SLOTS):
                    w = wts[a, b, c]
                    part = w * rows[a + c // 3][c % 3]
                    acc = part if acc is None else acc + part
                    if with_den:
                        tot = w if tot is None else tot + w
                num[a, pl.ds(b, 1), :] = row_sums(acc)
                if with_den:
                    den[a, pl.ds(b, 1), :] = row_sums(tot)
            return carry

        lax.fori_loop(low, high, body, 0)

    lax.fori_loop(1, cols_z - 1, inner, 0)
    pl.semaphore_wait(known, len(tellers))
    send_halo(ext0, 0, far_sides)
    rim_wait(ext0, h_recv.at[ITERS], rows_rim)
    middle = cols_z // 2
    lax.fori_loop(1, middle, outer, 0)
    whole_wait(got_first, g_recv.at[0])
    entries = 2 * n_gy * slots_out
    dest = n_near * guards
    code_rows = got_first[:, pl.ds(slots_out, slots_out), :].reshape(entries, PB)[:, :dest]
    lane = lax.broadcasted_iota(jnp.int32, (entries, dest), 1)
    wanted = (y * n_gz + half * n_near) * guards + lane
    hits = jnp.where(code_rows == wanted.astype(jnp.float32), 1.0, 0.0)
    chosen = jnp.transpose(hits).astype(jnp.bfloat16)
    onehot[...] = jnp.concatenate([chosen, chosen], axis=1)
    deliver(got_first[:, pl.ds(0, slots_out), :].reshape(entries, PB), 0)

    lax.fori_loop(middle, cols_z - 1, outer, 0)
    ends(False)

    def start_row(e, k):
        return ext0[e, k, pl.ds(3, 1), :]

    sums(start_row, True, 1, cols_z - 1)
    rim_wait(ext0, h_recv.at[0], far_rim)
    ends(True)
    sums(start_row, True, 0, 1)
    sums(start_row, True, cols_z - 1, cols_z)
    coef = gc_ref[0, 0, 0].reshape(rows_y, cols_z, PB)
    scale = 1.0 / (den[...] + coef + 1.0)

    for sweep in range(ITERS):
        base = num[...] - src_ref[0]
        whole_wait(got_buckets.at[sweep], r_recv.at[sweep])
        mine = buckets[sweep, near]
        for o in range(n_near - 1):
            mine = mine + got_buckets[sweep, o]
        new = (base + coef * mine.reshape(rows_y, cols_z, PB)) * scale
        if sweep == ITERS - 1:
            out_ref[0] = new
            break
        pden[...] = new.reshape(rows_y * cols_z, PB)
        interpolate(later.at[sweep])
        send_values(later.at[sweep], got.at[sweep], sweep + 1)
        press = pext.at[sweep]
        for a in range(rows_y):
            for b in range(cols_z):
                press[1 + a, 1 + b] = new[a, b : b + 1]
        send_halo(press, sweep + 1, sides)
        whole_wait(got.at[sweep], g_recv.at[sweep + 1])
        deliver(got[sweep].reshape(entries, PB), sweep + 1)
        rim_wait(press, h_recv.at[sweep + 1], rows_rim + far_rim)
        sums(lambda e, k: press[e, k], False, 0, cols_z)

    rim_wait(ext0, h_send.at[ITERS], rows_rim)
    rim_wait(ext0, h_send.at[0], far_rim)
    whole_wait(got_first, g_send.at[0])
    for sweep in range(ITERS):
        whole_wait(got_buckets.at[sweep], r_send.at[sweep])
        if sweep:
            rim_wait(pext.at[sweep - 1], h_send.at[sweep], rows_rim + far_rim)
            whole_wait(got.at[sweep - 1], g_send.at[sweep])


def local(n_gy, n_gz, *args):
    args = (jnp.swapaxes(args[0], 2, 3),) + args[1:]
    guard_coef, send_block = args[5], args[6]
    rows_y, cols_z = args[3].shape[1:3]
    guards = guard_coef.shape[3]
    slots_out = send_block.shape[3]
    n_near = n_gz // 2
    f32 = jnp.float32
    dma = pltpu.SemaphoreType.DMA((ITERS,))
    halo_dma = pltpu.SemaphoreType.DMA((ITERS + 1,))
    spaces = [pltpu.VMEM] * 6 + [pltpu.SMEM] * 4 + [pltpu.VMEM]
    return pl.pallas_call(
        functools.partial(kernel, n_gy, n_gz),
        out_shape=pltpu.VMEM((1, rows_y, cols_z, PB), f32),
        in_specs=[pl.BlockSpec(memory_space=pl.ANY)] * len(args),
        out_specs=pl.BlockSpec(memory_space=pltpu.VMEM),
        scratch_shapes=[space(a.shape, a.dtype) for space, a in zip(spaces, args)]
        + [
            pltpu.VMEM((rows_y + 2, cols_z + 2, 4, PB), f32),
            pltpu.VMEM((rows_y, cols_z, 8, PB), f32),
            pltpu.VMEM((ITERS - 1, rows_y + 2, cols_z + 2, 1, PB), f32),
            pltpu.VMEM((rows_y * cols_z, PB), f32),
            pltpu.VMEM((rows_y, cols_z, SLOTS, PB, PB), f32),
            pltpu.VMEM((SLOTS, rows_y, cols_z, PB), f32),
            pltpu.VMEM((2 * slots_out, PB), f32),
            pltpu.VMEM((ITERS - 1, slots_out, PB), f32),
            pltpu.VMEM((2 * n_gy, 2 * slots_out, PB), f32),
            pltpu.VMEM((ITERS - 1, 2 * n_gy, slots_out, PB), f32),
            pltpu.VMEM((ITERS, n_near, guards, PB), f32),
            pltpu.VMEM((ITERS, n_near - 1, guards, PB), f32),
            pltpu.VMEM((n_near * guards, 4 * n_gy * slots_out), jnp.bfloat16),
            pltpu.VMEM((rows_y, cols_z, PB), f32),
            pltpu.VMEM((rows_y, cols_z, PB), f32),
            halo_dma,
            halo_dma,
            dma,
            dma,
            dma,
            dma,
            pltpu.SemaphoreType.DMA((len(args),)),
            pltpu.SemaphoreType.REGULAR,
            pltpu.VMEM((ITERS, guards, PB), f32),
        ],
        compiler_params=pltpu.CompilerParams(
            collective_id=0, has_side_effects=True, vmem_limit_bytes=60 * 1024 * 1024
        ),
    )(*args)


def solution(mesh):
    placed = (
        P("grp", "gy", "gz", None, None),
        P("grp", "gy", "gz", None),
        P("grp", "gy", "gz"),
        P("grp", "gy", "gz", None),
        P("grp", "gy", "gz", None),
        P("grp", "gy", "gz", None, None),
        P("grp", "gy", "gz", None),
        P("grp", "gy", "gz", None),
        P("grp", "gy", "gz", None),
        P("grp", "gy", "gz"),
        P("grp", "gy", "gz", None, None, None),
    )
    return jax.shard_map(
        functools.partial(local, mesh.shape["gy"], mesh.shape["gz"]),
        mesh=mesh,
        in_specs=placed,
        out_specs=P("grp", "gy", "gz", None),
        check_vma=False,
    )
```

```python
import functools
import math

import jax
import jax.numpy as jnp
from jax import lax
from jax.experimental import pallas as pl
from jax.experimental.pallas import tpu as pltpu
from jax.sharding import PartitionSpec as P

PB = 128
SLOTS = 9
ITERS = 3
KERNEL_WIDTH = 0.5
MESH = pl.DeviceIdType.MESH
KAPPA = math.sqrt(1.0 / (KERNEL_WIDTH * math.log(2.0)))
OFF = -1.0e4


def kernel(
    n_gy,
    n_gz,
    *refs,
):
    sources, out_ref, held, rest = refs[:11], refs[11], refs[12:23], refs[23:]
    off_ref, list_ref, cnt_ref, src_ref, p_ref, gc_ref = held[:6]
    sb_ref, st_ref, sg_ref, sc_ref, interp_ref = held[6:]
    (
        ext0,
        own8,
        pext,
        pden,
        wts,
        mask,
        first,
        later,
        got_first,
        got,
        buckets,
        got_buckets,
        onehot,
        num,
        den,
        h_send,
        h_recv,
        g_send,
        g_recv,
        r_send,
        r_recv,
        in_sem,
        known,
    ) = rest
    g = lax.axis_index("grp")
    y = lax.axis_index("gy")
    z = lax.axis_index("gz")
    rows_y, cols_z = off_ref.shape[1], off_ref.shape[3]
    n_near = n_gz // 2
    half, near = z // n_near, lax.rem(z, n_near)
    guards = gc_ref.shape[3]
    slots_out = sb_ref.shape[3]

    def at(gg, dy, dz):
        return (gg, lax.rem(y + dy + n_gy, n_gy), lax.rem(z + dz + n_gz, n_gz))

    across = [o for o in (4, 5, 6, 7, 2, 3, 1, 0) if o < n_gy]
    stage1 = [(o, 1) for o in across[:6]] + [(o, 0) for o in across[:4]]
    stage1 += [(o, 1) for o in across[6:]] + [(o, 0) for o in across[4:]]
    stage2 = [o for o in (4, 5, 7, 6, 3, 2, 1) if o < n_near]

    def at1(o, f):
        return (1 - g, y ^ o, (half ^ f) * n_near + near)

    def at2(o):
        return (g, y, half * n_near + (near ^ o))

    copies = [
        pltpu.make_async_copy(src, dst, in_sem.at[i])
        for i, (src, dst) in enumerate(zip(sources, held))
    ]
    for i in (4, 6, 10):
        copies[i].start()
    barrier = pltpu.get_barrier_semaphore()
    farthest = n_near // 2
    beside = [at(g, 1, 0), at(g, -1, 0)]
    beside += [
        (g, lax.rem(y + a + n_gy, n_gy), (half ^ 1) * n_near + near) for a in (-1, 0, 1)
    ]
    people = [at1(*of) for of in stage1] + [at2(o) for o in stage2 if o != farthest] + beside
    tellers = beside + [at2(1)]
    for who in people:
        pl.semaphore_signal(barrier, inc=1, device_id=who, device_id_type=MESH)
    for i in (7, 8, 9, 0, 1, 2, 3, 5):
        copies[i].start()

    sides = []
    for dy in (-1, 0, 1):
        for dz in (-1, 0, 1):
            if (dy, dz) == (0, 0):
                continue
            ys = {-1: (1, 1), 0: (1, rows_y), 1: (rows_y, 1)}[dy]
            zs = {-1: (1, 1), 0: (1, cols_z), 1: (cols_z, 1)}[dz]
            yd = {-1: rows_y + 1, 0: 1, 1: 0}[dy]
            zd = {-1: cols_z + 1, 0: 1, 1: 0}[dz]
            sides.append((dy, dz, ys, zs, yd, zd))

    def send_halo(buf, sem, which):
        for dy, dz, ys, zs, yd, zd in which:
            pltpu.make_async_remote_copy(
                src_ref=buf.at[pl.ds(ys[0], ys[1]), pl.ds(zs[0], zs[1])],
                dst_ref=buf.at[pl.ds(yd, ys[1]), pl.ds(zd, zs[1])],
                send_sem=h_send.at[sem],
                recv_sem=h_recv.at[sem],
                device_id=at(g, dy, dz),
                device_id_type=MESH,
            ).start()

    rows_sides = [s for s in sides if s[1] == 0]
    far_sides = [s for s in sides if s[1] != 0]

    def rim_wait(buf, sem, blocks):
        part = buf.at[pl.ds(0, blocks // cols_z), pl.ds(0, cols_z)]
        pltpu.make_async_copy(part, part, sem).wait()

    rows_rim = 2 * cols_z
    far_rim = 2 * rows_y + 4

    def send_values(src, dst, sweep):
        for o, f in stage1:
            pltpu.make_async_remote_copy(
                src_ref=src,
                dst_ref=dst.at[2 * o + f],
                send_sem=g_send.at[sweep],
                recv_sem=g_recv.at[sweep],
                device_id=at1(o, f),
                device_id_type=MESH,
            ).start()

    def send_buckets(sweep):
        for o in stage2:
            pltpu.make_async_remote_copy(
                src_ref=buckets.at[sweep, near ^ o],
                dst_ref=got_buckets.at[sweep, o - 1],
                send_sem=r_send.at[sweep],
                recv_sem=r_recv.at[sweep],
                device_id=at2(o),
                device_id_type=MESH,
            ).start()

    def whole_wait(ref, sem):
        pltpu.make_async_copy(ref, ref, sem).wait()

    row_id = lax.broadcasted_iota(jnp.int32, (PB, PB), 0)
    lane_id = lax.broadcasted_iota(jnp.int32, (PB, PB), 1)
    eye = row_id == lane_id

    def row_sums(acc):
        total = jnp.sum(acc, axis=1, keepdims=True)
        return jnp.sum(jnp.where(eye, total, 0.0), axis=0, keepdims=True)

    def interpolate(dst):
        for s in range(slots_out):
            press = pden[pl.ds(sb_ref[0, 0, 0, s], 1), :]
            dst[pl.ds(s, 1), :] = row_sums(interp_ref[0, 0, 0, s] * press)

    for i in (4, 6):
        copies[i].wait()
    for a in range(rows_y):
        pden[pl.ds(a * cols_z, cols_z), :] = p_ref[0, a]
    copies[10].wait()
    interpolate(first)
    for i in (7, 8, 9):
        copies[i].wait()
    codes = jnp.full((slots_out, PB), -1, jnp.int32)
    slot_row = lax.broadcasted_iota(jnp.int32, (slots_out, PB), 0)
    for s in range(slots_out):
        codes = jnp.where(slot_row == s, st_ref[0, 0, 0, s] * guards + sg_ref[0, 0, 0, s], codes)
    codes = jnp.where(slot_row < sc_ref[0, 0, 0], codes, -1)
    first[pl.ds(slots_out, slots_out), :] = codes.astype(jnp.float32)

    pl.semaphore_wait(barrier, len(people))
    for who in tellers:
        pl.semaphore_signal(known, inc=1, device_id=who, device_id_type=MESH)
    send_values(first, got_first, 0)

    copies[0].wait()
    for a in range(rows_y):
        for k in range(3):
            scaled = (off_ref[0, a, k] - 0.5) * (2.0 * KAPPA)
            for b in range(cols_z):
                ext0[1 + a, 1 + b, pl.ds(k, 1), :] = scaled[b : b + 1]
                own8[a, b, pl.ds(k, 1), :] = 0.5 * scaled[b : b + 1]
        for b in range(cols_z):
            ext0[1 + a, 1 + b, pl.ds(3, 1), :] = p_ref[0, a, pl.ds(b, 1), :]
    send_halo(ext0, ITERS, rows_sides)
    for i in (1, 2, 3, 5):
        copies[i].wait()

    for a in range(rows_y):
        lanes = lax.broadcasted_iota(jnp.int32, (cols_z, cols_z), 1)
        subs = lax.broadcasted_iota(jnp.int32, (cols_z, cols_z), 0)
        counts = jnp.sum(
            jnp.where(lanes == subs, cnt_ref[0, pl.ds(a, 1), :], 0).astype(jnp.float32),
            axis=1,
            keepdims=True,
        )
        places = lax.broadcasted_iota(jnp.int32, (cols_z, SLOTS), 1).astype(jnp.float32)
        for c in range(SLOTS):
            hit = (list_ref[0, a] == c) & (places < counts)
            active = jnp.sum(jnp.where(hit, 1.0, 0.0), axis=1, keepdims=True)
            mask[c, a] = jnp.broadcast_to((1.0 - active) * OFF, (cols_z, PB))

    def own_columns(a, b):
        cols = jnp.transpose(own8[a, b])
        cx = jnp.broadcast_to(cols[:, 0:1], (PB, PB))
        cy = jnp.broadcast_to(cols[:, 1:2], (PB, PB))
        cz = jnp.broadcast_to(cols[:, 2:3], (PB, PB))
        return cx, cy, cz, -(cx * cx + cy * cy + cz * cz)

    def make_weights(a, b, pairs):
        cx, cy, cz, cn = own_columns(a, b)
        for dy, dz in pairs:
            c = 3 * (dy + 1) + (dz + 1)
            near = ext0[1 + a + dy, 1 + b + dz]
            rx = near[0:1]
            ry = near[1:2] + 2.0 * KAPPA * dy
            rz = near[2:3] + 2.0 * KAPPA * dz
            rn = mask[c, a, pl.ds(b, 1), :] - 0.25 * (rx * rx + ry * ry + rz * rz)
            wts[a, b, c] = jnp.exp2((cn + rn) + (cx * rx + cy * ry) + cz * rz)

    all_dz = (-1, 0, 1)

    def inner(b, carry):
        for a in range(rows_y):
            dys = [dy for dy in (-1, 0, 1) if 0 <= a + dy < rows_y]
            make_weights(a, b, [(dy, dz) for dy in dys for dz in all_dz])
        return carry

    def outer(b, carry):
        for a in range(rows_y):
            dys = [dy for dy in (-1, 0, 1) if not 0 <= a + dy < rows_y]
            make_weights(a, b, [(dy, dz) for dy in dys for dz in all_dz])
        return carry

    def ends(far):
        for b, out in ((0, -1), (cols_z - 1, 1)):
            for a in range(rows_y):
                dzs = [dz for dz in all_dz if (dz == out) == far]
                make_weights(a, b, [(dy, dz) for dy in (-1, 0, 1) for dz in dzs])

    def deliver(values, sweep):
        hi = values.astype(jnp.bfloat16)
        low = (values - hi.astype(jnp.float32)).astype(jnp.bfloat16)
        both = jnp.concatenate([hi, low], axis=0)
        total = jnp.dot(onehot[...], both, preferred_element_type=jnp.float32)
        buckets[sweep] = total.reshape(n_near, guards, PB)
        send_buckets(sweep)

    def sums(near_row, with_den, low, high):
        def body(b, carry):
            rows = [[near_row(e, b + k) for k in range(3)] for e in range(rows_y + 2)]
            for a in range(rows_y):
                acc = None
                tot = None
                for c in range(SLOTS):
                    w = wts[a, b, c]
                    part = w * rows[a + c // 3][c % 3]
                    acc = part if acc is None else acc + part
                    if with_den:
                        tot = w if tot is None else tot + w
                num[a, pl.ds(b, 1), :] = row_sums(acc)
                if with_den:
                    den[a, pl.ds(b, 1), :] = row_sums(tot)
            return carry

        lax.fori_loop(low, high, body, 0)

    lax.fori_loop(1, cols_z - 1, inner, 0)
    pl.semaphore_wait(known, len(tellers))
    send_halo(ext0, 0, far_sides)
    rim_wait(ext0, h_recv.at[ITERS], rows_rim)
    middle = cols_z // 2
    lax.fori_loop(1, middle, outer, 0)
    whole_wait(got_first, g_recv.at[0])
    entries = 2 * n_gy * slots_out
    dest = n_near * guards
    code_rows = got_first[:, pl.ds(slots_out, slots_out), :].reshape(entries, PB)[:, :dest]
    lane = lax.broadcasted_iota(jnp.int32, (entries, dest), 1)
    wanted = (y * n_gz + half * n_near) * guards + lane
    hits = jnp.where(code_rows == wanted.astype(jnp.float32), 1.0, 0.0)
    chosen = jnp.transpose(hits).astype(jnp.bfloat16)
    onehot[...] = jnp.concatenate([chosen, chosen], axis=1)
    deliver(got_first[:, pl.ds(0, slots_out), :].reshape(entries, PB), 0)

    lax.fori_loop(middle, cols_z - 1, outer, 0)
    ends(False)

    def start_row(e, k):
        return ext0[e, k, pl.ds(3, 1), :]

    sums(start_row, True, 1, cols_z - 1)
    rim_wait(ext0, h_recv.at[0], far_rim)
    ends(True)
    sums(start_row, True, 0, 1)
    sums(start_row, True, cols_z - 1, cols_z)
    coef = gc_ref[0, 0, 0].reshape(rows_y, cols_z, PB)
    scale = 1.0 / (den[...] + coef + 1.0)
    weight = coef * scale

    for sweep in range(ITERS):
        base = (num[...] - src_ref[0]) * scale
        own = buckets[sweep, near]
        whole_wait(got_buckets.at[sweep], r_recv.at[sweep])
        mine = own
        for o in range(n_near - 1):
            mine = mine + got_buckets[sweep, o]
        new = base + weight * mine.reshape(rows_y, cols_z, PB)
        if sweep == ITERS - 1:
            out_ref[0] = new
            break
        pden[...] = new.reshape(rows_y * cols_z, PB)
        interpolate(later.at[sweep])
        send_values(later.at[sweep], got.at[sweep], sweep + 1)
        press = pext.at[sweep]
        for a in range(rows_y):
            for b in range(cols_z):
                press[1 + a, 1 + b] = new[a, b : b + 1]
        send_halo(press, sweep + 1, sides)
        whole_wait(got.at[sweep], g_recv.at[sweep + 1])
        deliver(got[sweep].reshape(entries, PB), sweep + 1)
        rim_wait(press, h_recv.at[sweep + 1], rows_rim + far_rim)
        sums(lambda e, k: press[e, k], False, 0, cols_z)

    rim_wait(ext0, h_send.at[ITERS], rows_rim)
    rim_wait(ext0, h_send.at[0], far_rim)
    whole_wait(got_first, g_send.at[0])
    for sweep in range(ITERS):
        whole_wait(got_buckets.at[sweep], r_send.at[sweep])
        if sweep:
            rim_wait(pext.at[sweep - 1], h_send.at[sweep], rows_rim + far_rim)
            whole_wait(got.at[sweep - 1], g_send.at[sweep])


def local(n_gy, n_gz, *args):
    args = (jnp.swapaxes(args[0], 2, 3),) + args[1:]
    guard_coef, send_block = args[5], args[6]
    rows_y, cols_z = args[3].shape[1:3]
    guards = guard_coef.shape[3]
    slots_out = send_block.shape[3]
    n_near = n_gz // 2
    f32 = jnp.float32
    dma = pltpu.SemaphoreType.DMA((ITERS,))
    halo_dma = pltpu.SemaphoreType.DMA((ITERS + 1,))
    spaces = [pltpu.VMEM] * 6 + [pltpu.SMEM] * 4 + [pltpu.VMEM]
    return pl.pallas_call(
        functools.partial(kernel, n_gy, n_gz),
        out_shape=pltpu.VMEM((1, rows_y, cols_z, PB), f32),
        in_specs=[pl.BlockSpec(memory_space=pl.ANY)] * len(args),
        out_specs=pl.BlockSpec(memory_space=pltpu.VMEM),
        scratch_shapes=[space(a.shape, a.dtype) for space, a in zip(spaces, args)]
        + [
            pltpu.VMEM((rows_y + 2, cols_z + 2, 4, PB), f32),
            pltpu.VMEM((rows_y, cols_z, 8, PB), f32),
            pltpu.VMEM((ITERS - 1, rows_y + 2, cols_z + 2, 1, PB), f32),
            pltpu.VMEM((rows_y * cols_z, PB), f32),
            pltpu.VMEM((rows_y, cols_z, SLOTS, PB, PB), f32),
            pltpu.VMEM((SLOTS, rows_y, cols_z, PB), f32),
            pltpu.VMEM((2 * slots_out, PB), f32),
            pltpu.VMEM((ITERS - 1, slots_out, PB), f32),
            pltpu.VMEM((2 * n_gy, 2 * slots_out, PB), f32),
            pltpu.VMEM((ITERS - 1, 2 * n_gy, slots_out, PB), f32),
            pltpu.VMEM((ITERS, n_near, guards, PB), f32),
            pltpu.VMEM((ITERS, n_near - 1, guards, PB), f32),
            pltpu.VMEM((n_near * guards, 4 * n_gy * slots_out), jnp.bfloat16),
            pltpu.VMEM((rows_y, cols_z, PB), f32),
            pltpu.VMEM((rows_y, cols_z, PB), f32),
            halo_dma,
            halo_dma,
            dma,
            dma,
            dma,
            dma,
            pltpu.SemaphoreType.DMA((len(args),)),
            pltpu.SemaphoreType.REGULAR,
        ],
        compiler_params=pltpu.CompilerParams(
            collective_id=0, has_side_effects=True, vmem_limit_bytes=60 * 1024 * 1024
        ),
    )(*args)


def solution(mesh):
    placed = (
        P("grp", "gy", "gz", None, None),
        P("grp", "gy", "gz", None),
        P("grp", "gy", "gz"),
        P("grp", "gy", "gz", None),
        P("grp", "gy", "gz", None),
        P("grp", "gy", "gz", None, None),
        P("grp", "gy", "gz", None),
        P("grp", "gy", "gz", None),
        P("grp", "gy", "gz", None),
        P("grp", "gy", "gz"),
        P("grp", "gy", "gz", None, None, None),
    )
    return jax.shard_map(
        functools.partial(local, mesh.shape["gy"], mesh.shape["gz"]),
        mesh=mesh,
        in_specs=placed,
        out_specs=P("grp", "gy", "gz", None),
        check_vma=False,
    )
```
